32 devices in a mesh: batch: 4 (over y, x), wide: 8 (over z, core).
Axes of the slice: x: 2, y: 2, z: 4, core: 2. Of those that a mesh axis runs over, the one named last changes fastest.
Arguments:
- inputs: bfloat16 [64, 1024, 256], P('batch', 'wide'), may hold values from -6 to 6
- lengths: int32 [64], P('batch'), may hold values from 256 to 1024, as said below
- ln1_gain: float32 [2, 256], replicated, may hold values from 0.5 to 1.5
- ln1_bias: float32 [2, 256], replicated, may hold values from -1.5 to 1.5
- w_qkv: bfloat16 [2, 256, 768], replicated, may hold values from -0.5 to 0.5
- w_out: bfloat16 [2, 256, 256], replicated, may hold values from -1.5 to 1.5
- ln2_gain: float32 [2, 256], replicated, may hold values from 0.5 to 1.5
- ln2_bias: float32 [2, 256], replicated, may hold values from -1.5 to 1.5
- w_up: bfloat16 [2, 256, 1024], replicated, may hold values from -0.375 to 0.375
- w_down: bfloat16 [2, 1024, 256], replicated, may hold values from -0.25 to 0.25
- cotangent: bfloat16 [64, 1024, 256], P('batch', 'wide'), may hold values from -6 to 6
Outputs:
- outputs: bfloat16 [64, 1024, 256], P('batch', 'wide')
- grad_inputs: float32 [64, 1024, 256], P('batch', 'wide')
- grad_ln1_gain: float32 [2, 256], replicated
- grad_ln1_bias: float32 [2, 256], replicated
- grad_w_qkv: float32 [2, 256, 768], replicated
- grad_w_out: float32 [2, 256, 256], replicated
- grad_ln2_gain: float32 [2, 256], replicated
- grad_ln2_bias: float32 [2, 256], replicated
- grad_w_up: float32 [2, 256, 1024], replicated
- grad_w_down: float32 [2, 1024, 256], replicated
The draws below stay inside these ranges and needn't reach their ends.
Inputs may be any that keep to these rules, and one draw needn't show every extreme that they name: `lengths`: in each aligned group of 16 sequences one has length 1024.
All inputs are finite; a program needn't handle non-finite values.
Results may differ from the reference program's by a relative error of at most 0.018.
The reference program's roundings to bfloat16 on the way count: a program that leaves them out, or rounds other values in their place, can miss the bound.
Values may be sent and summed in bfloat16 or wider, within the bound.
A program may use at most 384 MiB of HBM per device.

```python
import jax
import jax.numpy as jnp
from jax import lax

D = 256
FF = 1024
WINDOW = 128
LAYERS = 2
SEQ_DEV = 16
SEQ_LEN = 1024
SEQS = 64


def draw_lengths(key, part):
    key = jax.random.fold_in(key, 7)
    first_key, second_key = jax.random.split(key)
    drawn = jax.random.randint(first_key, (SEQS // SEQ_DEV, SEQ_DEV), SEQ_LEN // 4, SEQ_LEN + 1, dtype=jnp.int32)
    chosen = jax.random.randint(second_key, (SEQS // SEQ_DEV, 1), 0, SEQ_DEV, dtype=jnp.int32)
    longest = jnp.arange(SEQ_DEV, dtype=jnp.int32)[None, :] == chosen
    return jnp.where(longest, SEQ_LEN, drawn).reshape(SEQS).astype(jnp.int32)


def level_of(own_key, dims, shards, low, high):
    def one(dim, parts):
        draws = jax.random.uniform(jax.random.fold_in(jax.random.fold_in(own_key, 6), dim), (parts,), jnp.float32, low / len(shards), high / len(shards))
        return jnp.repeat(jnp.exp(draws), dims[dim] // parts).reshape((-1,) + (1,) * (len(dims) - dim - 1))

    factor_of = one(*shards[0])
    for cut in shards[1:]:
        factor_of = factor_of * one(*cut)
    return factor_of


def noise(own_key, dims, deviation, reach, pieces=(), kind=jnp.bfloat16):
    level = level_of(own_key, dims, pieces, -0.22, 0.18) if pieces else 1.0
    entries = jax.random.normal(own_key, dims, jnp.float32) * deviation * level
    return jnp.minimum(jnp.maximum(entries, -reach), reach).astype(kind)


def setup_inputs(seed: int = 0) -> dict:
    arg_keys = jax.random.split(jax.random.key(seed), 12)
    return {
        "inputs": noise(arg_keys[0], (SEQS, SEQ_LEN, D), 1.0, 6.0, ((0, 4), (1, 8))),
        "lengths": draw_lengths(jax.random.fold_in(arg_keys[11], 71), 0),
        "ln1_gain": jnp.clip(1.0 + 0.1 * jax.random.normal(arg_keys[2], (LAYERS, D), jnp.float32), 0.5, 1.5),
        "ln1_bias": noise(arg_keys[3], (LAYERS, D), 0.3, 1.5, (), jnp.float32),
        "w_qkv": noise(arg_keys[4], (LAYERS, D, 3 * D), (D // 2) ** -0.5, 0.5),
        "w_out": noise(arg_keys[5], (LAYERS, D, D), (D // 16) ** -0.5, 1.5),
        "ln2_gain": jnp.clip(1.0 + 0.1 * jax.random.normal(arg_keys[6], (LAYERS, D), jnp.float32), 0.5, 1.5),
        "ln2_bias": noise(arg_keys[7], (LAYERS, D), 0.3, 1.5, (), jnp.float32),
        "w_up": noise(arg_keys[8], (LAYERS, D, FF), D ** -0.5, 0.375),
        "w_down": noise(arg_keys[9], (LAYERS, FF, D), (FF // 2) ** -0.5, 0.25),
        "cotangent": noise(arg_keys[10], (SEQS, SEQ_LEN, D), 1.0, 6.0, ((0, 4), (1, 8))),
    }


@jax.custom_vjp
def low(v):
    return lax.optimization_barrier(v.astype(jnp.bfloat16)).astype(jnp.float32)

@jax.custom_vjp
def low_back(v):
    return v

def low_keep(v):
    return (low(v), None)

def low_pass(kept, grad):
    return (grad,)

def back_keep(v):
    return (v, None)

def back_low(kept, grad):
    return (low(grad),)
low.defvjp(low_keep, low_pass)
low_back.defvjp(back_keep, back_low)
highest = lax.Precision.HIGHEST
big_negative = -1e+30

def layer_norm(values, gain, shift):
    center = values - lax.optimization_barrier(jnp.mean(values, axis=-1, keepdims=True))
    spread = lax.optimization_barrier(jnp.mean(center * center, axis=-1, keepdims=True))
    return center * lax.rsqrt(spread + 1e-05) * gain + shift

def masked_softmax(scores, allowed, axis_pick):
    masked = jnp.where(allowed, scores, big_negative)
    row_peak = lax.optimization_barrier(jnp.max(masked, axis=axis_pick, keepdims=True))
    powered = jnp.where(allowed, jnp.exp(masked - row_peak), 0.0)
    return powered / lax.optimization_barrier(jnp.sum(powered, axis=axis_pick, keepdims=True))

def local_attention(queries, key_rows, value_rows, seq_lengths):
    groups, seq_len, head_size = queries.shape
    block_count = seq_len // WINDOW
    score_scale = float(head_size) ** (-0.5)
    query_blocks = queries.reshape(groups, block_count, WINDOW, head_size)

    def with_earlier(source):
        blocks = source.reshape(groups, block_count, WINDOW, head_size)
        earlier = jnp.concatenate([jnp.zeros_like(blocks[:, :1]), blocks[:, :-1]], axis=1)
        return jnp.concatenate([earlier, blocks], axis=2)
    key_part = with_earlier(key_rows)
    value_part = with_earlier(value_rows)
    raw_scores = jnp.einsum('gnrd,gncd->gnrc', query_blocks, key_part, precision=highest)
    scores = low_back(raw_scores * score_scale)
    block_start = jnp.arange(block_count, dtype=jnp.int32) * WINDOW
    query_pos = block_start[:, None, None] + jnp.arange(WINDOW, dtype=jnp.int32)[None, :, None]
    key_pos = block_start[:, None, None] - WINDOW + jnp.arange(2 * WINDOW, dtype=jnp.int32)[None, None, :]
    allowed = (key_pos <= query_pos) & (key_pos > query_pos - WINDOW) & (key_pos >= 0)
    allowed = allowed[None] & ((key_pos[None] < seq_lengths[:, None, None, None]) | (key_pos == query_pos)[None])
    weights = low(masked_softmax(scores, allowed, 3))
    result_rows = jnp.einsum('gnrc,gncd->gnrd', weights, value_part, precision=highest)
    return result_rows.reshape(groups, seq_len, head_size)

def strided_attention(queries, key_rows, value_rows, seq_lengths):
    groups, seq_len, head_size = queries.shape
    block_count = seq_len // WINDOW
    score_scale = float(head_size) ** (-0.5)
    query_blocks = queries.reshape(groups, block_count, WINDOW, head_size)
    key_blocks = key_rows.reshape(groups, block_count, WINDOW, head_size)
    value_blocks = value_rows.reshape(groups, block_count, WINDOW, head_size)
    raw_scores = jnp.einsum('gnod,gmod->gnmo', query_blocks, key_blocks, precision=highest)
    scores = low_back(raw_scores * score_scale)
    block_ids = jnp.arange(block_count, dtype=jnp.int32)
    query_block = block_ids[:, None, None]
    key_block = block_ids[None, :, None]
    key_pos = key_block * WINDOW + jnp.arange(WINDOW, dtype=jnp.int32)[None, None, :]
    allowed = (key_block <= query_block)[None] & ((key_pos[None] < seq_lengths[:, None, None, None]) | (key_block == query_block)[None])
    weights = low(masked_softmax(scores, allowed, 2))
    result_rows = jnp.einsum('gnmo,gmod->gnod', weights, value_blocks, precision=highest)
    return result_rows.reshape(groups, seq_len, head_size)

def one_layer(stream, seq_lengths, layer_weights):
    gain_one, shift_one, w_pack, w_mix, gain_two, shift_two, w_expand, w_shrink = layer_weights
    groups, seq_len, model_width = stream.shape
    normed = low(layer_norm(stream, gain_one, shift_one))
    packed = low(low_back(jnp.einsum('gld,de->gle', normed, w_pack, precision=highest)))
    packed = packed.reshape(groups, seq_len, 3, 2, model_width // 2)
    near_out = local_attention(packed[:, :, 0, 0], packed[:, :, 1, 0], packed[:, :, 2, 0], seq_lengths)
    far_out = strided_attention(packed[:, :, 0, 1], packed[:, :, 1, 1], packed[:, :, 2, 1], seq_lengths)
    mixed_heads = low(low_back(jnp.concatenate([near_out, far_out], axis=-1)))
    stream = stream + low_back(jnp.einsum('gld,de->gle', mixed_heads, w_mix, precision=highest))
    normed_two = low(layer_norm(stream, gain_two, shift_two))
    hidden = low_back(jnp.einsum('gld,df->glf', normed_two, w_expand, precision=highest))
    active = low(jax.nn.gelu(hidden))
    return stream + low_back(jnp.einsum('glf,fd->gld', active, w_shrink, precision=highest))

def forward(stream, seq_lengths, parameters):
    for layer_index in range(LAYERS):
        stream = one_layer(stream, seq_lengths, tuple((member[layer_index] for member in parameters)))
    return stream

def reference(inputs, lengths, ln1_gain, ln1_bias, w_qkv, w_out, ln2_gain, ln2_bias, w_up, w_down, cotangent):
    parameters = tuple((member.astype(jnp.float32) for member in (ln1_gain, ln1_bias, w_qkv, w_out, ln2_gain, ln2_bias, w_up, w_down)))
    streams = inputs.astype(jnp.float32).reshape(SEQS, 1, SEQ_LEN, D)
    grad_streams = cotangent.astype(jnp.float32).reshape(SEQS, 1, SEQ_LEN, D)
    length_rows = lengths.reshape(SEQS, 1)

    def scan_step(totals, slices):
        stream, seq_lengths, grad_out = slices

        def closed(stream_in, params_in):
            return forward(stream_in, seq_lengths, params_in)
        result, pull_back = jax.vjp(closed, stream, parameters)
        grad_stream, grad_params = pull_back(grad_out)

        def add_pair(first_term, second_term):
            return first_term + second_term
        totals = jax.tree.map(add_pair, totals, grad_params)
        return (totals, (result, grad_stream))
    zeros_start = jax.tree.map(jnp.zeros_like, parameters)
    totals, (results, grad_rows) = lax.scan(scan_step, zeros_start, (streams, length_rows, grad_streams))
    outputs = results.reshape(SEQS, SEQ_LEN, D).astype(jnp.bfloat16)
    grad_inputs = grad_rows.reshape(SEQS, SEQ_LEN, D)
    return (outputs, grad_inputs, totals[0], totals[1], totals[2], totals[3], totals[4], totals[5], totals[6], totals[7])
```

```python
import types

import jax
import jax.numpy as jnp
from jax import lax
from jax.experimental import pallas as pl
from jax.experimental.pallas import tpu as pltpu
from jax.sharding import PartitionSpec as P

MESH = pl.DeviceIdType.MESH
F32, BF16 = jnp.float32, jnp.bfloat16
HEAD = 128
WINDOW = 128
GROUP = 16
TILE = 4
PIECE = 32
CHUNK = 256
ROOMY = 8
AT_ONCE = 4
Q_NEAR, Q_FAR, K_NEAR, K_FAR, V_NEAR, V_FAR = (slice(i * HEAD, (i + 1) * HEAD) for i in range(6))
FAR = 1 << 20
MASKED = -1e30
LOG2E = 1.4426950408889634
GELU_A = 0.7978845608028654
GELU_B = GELU_A * 0.044715


def dot(a, b):
    return lax.dot_general(a, b, (((1,), (0,)), ((), ())), preferred_element_type=F32)


def dot_nt(a, b):
    return lax.dot_general(a, b, (((1,), (1,)), ((), ())), preferred_element_type=F32)


def dot_tn(a, b):
    return lax.dot_general(a, b, (((0,), (0,)), ((), ())), preferred_element_type=F32)


def flat(v):
    return v.reshape(-1, v.shape[-1])


def blocks(v):
    return v.reshape(-1, WINDOW, v.shape[-1])


def normalize(x):
    center = x - jnp.mean(x, axis=-1, keepdims=True)
    inverse = lax.rsqrt(jnp.mean(center * center, axis=-1, keepdims=True) + 1e-05)
    return center * inverse, inverse


def norm_back(grad, hat, inverse, gain):
    scaled = grad * gain
    first = jnp.mean(scaled, axis=-1, keepdims=True)
    second = jnp.mean(scaled * hat, axis=-1, keepdims=True)
    return inverse * (scaled - first - hat * second)


def row_sums(v):
    return jnp.sum(v.reshape(-1, 8, v.shape[-1]), axis=0)


def pieces_of(rows):
    return [slice(i, i + PIECE) for i in range(0, rows, PIECE)]


def weights_of(scores, order, limit, factor):
    parts = []
    for r in pieces_of(scores.shape[0]):
        masked = jnp.where(order[r] < limit, scores[r], MASKED)
        peak = jnp.max(masked, axis=1, keepdims=True)
        powered = jnp.exp2((masked - peak) * factor)
        parts.append((powered * (1.0 / jnp.sum(powered, axis=1, keepdims=True))).astype(BF16))
    return jnp.concatenate(parts, axis=0)


def gelu_pair(h):
    square = h * h
    q = 0.5 * jnp.tanh(h * (GELU_B * square + GELU_A)) + 0.5
    g = h * q
    slope = q + g * (1.0 - q) * (6.0 * GELU_B * square + 2.0 * GELU_A)
    return g.astype(BF16), slope.astype(BF16)


def plan(nb, nw, ns, nblk, width, hidden, layers):
    total = ns * nblk
    far_rows = nblk * GROUP
    rows = 12 * CHUNK
    pieces = {}

    def vmem(name, dims, kind):
        pieces[name] = pltpu.VMEM(dims, kind)

    def sems(name, *dims):
        pieces[name] = pltpu.SemaphoreType.DMA(dims)

    vmem("x_in", (total, WINDOW, width), BF16)
    vmem("cot_in", (total, WINDOW, width), BF16)
    vmem("w_qkv", (layers, width, 3 * width), BF16)
    vmem("w_out", (layers, width, width), BF16)
    vmem("w_up", (layers, width, hidden), BF16)
    vmem("w_down", (layers, hidden, width), BF16)
    vmem("a1", (layers, nblk, WINDOW, width), BF16)
    vmem("a2", (layers, nblk, WINDOW, width), BF16)
    vmem("qkv", (layers, nblk, WINDOW, 3 * width), BF16)
    vmem("heads", (layers, nblk, WINDOW, width), BF16)
    vmem("near_p", (layers, nblk, WINDOW, 2 * WINDOW), BF16)
    vmem("far_p", (layers, WINDOW // GROUP, far_rows, far_rows), BF16)
    vmem("act", (layers, nblk, WINDOW, hidden), BF16)
    vmem("slope", (layers, nblk, WINDOW, hidden), BF16)
    vmem("stats", (nblk, WINDOW, WINDOW), F32)
    vmem("dx", (nblk, WINDOW, width), F32)
    vmem("df", (nblk, WINDOW, width), BF16)
    vmem("dm", (nblk, WINDOW, width), BF16)
    vmem("do", (nblk, WINDOW, width), BF16)
    vmem("near_ds", (nblk, WINDOW, 2 * WINDOW), BF16)
    vmem("near_dq", (nblk, WINDOW, HEAD), BF16)
    vmem("df_t", (width, nblk * WINDOW), BF16)
    vmem("heads_t", (width, nblk * WINDOW), BF16)
    if nblk <= ROOMY:
        vmem("a1_t", (layers, width, nblk * WINDOW), BF16)
        vmem("a2_t", (layers, width, nblk * WINDOW), BF16)
        vmem("w_qkv_t", (layers, 3 * width, width), BF16)
        vmem("w_out_t", (layers, width, width), BF16)
        vmem("w_up_t", (layers, hidden, width), BF16)
        vmem("w_down_t", (layers, width, hidden), BF16)
    vmem("near_order", (2, WINDOW, 2 * WINDOW), jnp.int32)
    vmem("far_order", (far_rows, far_rows), jnp.int32)
    vmem("sums", (layers, 4, 8, width), F32)
    vmem("grad", (layers, rows, CHUNK), F32)
    vmem("final", (layers, rows, CHUNK), BF16)
    vmem("got_core", (layers, rows // 2, CHUNK), BF16)
    vmem("got_batch", (layers, nb, rows // 2 // nb, CHUNK), BF16)
    vmem("got_pair", (layers, rows // 4 // nb, CHUNK), BF16)
    top = max(nw.bit_length() - 3, 1)
    vmem("got_top", (layers, top, rows // 4 // nb, CHUNK), BF16)
    vmem("put_core", (hidden, CHUNK), BF16)
    vmem("put_batch", (hidden, CHUNK), BF16)
    vmem("put_pair", (rows // 4 // nb, CHUNK), BF16)
    vmem("put_top", (top, rows // 4 // nb, CHUNK), BF16)
    vmem("norm_all", (nw, 4 * layers, width), F32)
    vmem("norm_batch", (nb, 4 * layers, width), F32)
    for name in ("in", "cot", "out", "gi"):
        sems(name + "_s", ns, nw)
        sems(name + "_r", ns, nw)
    sems("own", 4, ns)
    sems("load", 4)
    sems("save", layers, 2)
    for name, count in (("core", 1), ("batch", nb), ("pair", 1), ("top", top), ("pair_back", 1), ("batch_back", nb), ("core_back", 1)):
        sems(name + "_s", layers, 2, count)
        sems(name + "_r", layers, 2, count)
    sems("norm_all_s", nw)
    sems("norm_all_r", nw)
    sems("norm_batch_s", nb)
    sems("norm_batch_r", nb)
    return pieces


def kernel(nb, nw, ns, names, *refs):
    (lens, x_hbm, cot_hbm, gain1, bias1, gain2, bias2, wq_hbm, wo_hbm, wu_hbm, wd_hbm,
     out_hbm, gi_hbm, grads_hbm, norm_out) = refs[:15]
    m = types.SimpleNamespace(**dict(zip(names, refs[15:])))
    layers, width = gain1.shape
    hidden = wu_hbm.shape[2]
    per = x_hbm.shape[2]
    nblk = nw * per
    tiles = nblk // TILE
    groups = WINDOW // GROUP
    near_each = nblk // groups
    scale = float(HEAD) ** (-0.5)
    factor = scale * LOG2E
    me = lax.axis_index("wide")
    mb = lax.axis_index("batch")

    barrier = pltpu.get_barrier_semaphore()
    for k in range(1, nw):
        pl.semaphore_signal(barrier, inc=1, device_id=(mb, lax.rem(me + k, nw)), device_id_type=MESH)
    for k in range(1, nb):
        pl.semaphore_signal(barrier, inc=1, device_id=(lax.rem(mb + k, nb), me), device_id_type=MESH)
    pl.semaphore_wait(barrier, nw + nb - 2)

    def partner(k):
        place = me
        for bit in range(nw.bit_length() - 1):
            size = 2**bit
            if k & size:
                place = place + size - 2 * size * lax.rem(me // size, 2)
        return place

    far = [nw // 2 + k for k in range(nw // 2)]
    close = [k for k in range(nw // 2 - 1, 0, -1)]
    turns = [turn for pair in zip(far, close) for turn in pair] + [far[-1]]

    def gather_copy(src, dst, send, recv, s, other, owner):
        return pltpu.make_async_remote_copy(
            src_ref=src.at[other, s],
            dst_ref=dst.at[pl.ds(s * nblk + owner * per, per)],
            send_sem=send.at[s, other],
            recv_sem=recv.at[s, owner],
            device_id=(mb, other),
            device_id_type=MESH,
        )

    def gather_own(src, dst, which, s):
        return pltpu.make_async_copy(
            src.at[me, s], dst.at[pl.ds(s * nblk + me * per, per)], m.own.at[which, s]
        )

    def gather_start(src, dst, send, recv, which, s):
        for k in turns:
            gather_copy(src, dst, send, recv, s, partner(k), me).start()
        gather_own(src, dst, which, s).start()

    def gather_wait(src, dst, send, recv, which, s):
        for k in range(1, nw):
            other = partner(k)
            gather_copy(src, dst, send, recv, s, other, other).wait_recv()
        gather_own(src, dst, which, s).wait()

    def gather_end(src, dst, send, recv, s):
        for k in range(1, nw):
            gather_copy(src, dst, send, recv, s, partner(k), me).wait_send()

    def scatter_copy(src, dst, send, recv, s, other, owner):
        return pltpu.make_async_remote_copy(
            src_ref=src.at[pl.ds(s * nblk + other * per, per)],
            dst_ref=dst.at[owner, s],
            send_sem=send.at[s, other],
            recv_sem=recv.at[s, owner],
            device_id=(mb, other),
            device_id_type=MESH,
        )

    def scatter_own(src, dst, which, s):
        return pltpu.make_async_copy(
            src.at[pl.ds(s * nblk + me * per, per)], dst.at[me, s], m.own.at[which, s]
        )

    def scatter_start(src, dst, send, recv, which, s):
        for k in turns:
            scatter_copy(src, dst, send, recv, s, partner(k), me).start()
        scatter_own(src, dst, which, s).start()

    def scatter_end(src, dst, send, recv, which, s):
        for k in range(1, nw):
            scatter_copy(src, dst, send, recv, s, partner(k), me).wait_send()
        for k in range(1, nw):
            other = partner(k)
            scatter_copy(src, dst, send, recv, s, other, other).wait_recv()
        scatter_own(src, dst, which, s).wait()

    ins = (x_hbm, m.x_in, m.in_s, m.in_r)
    cots = (cot_hbm, m.cot_in, m.cot_s, m.cot_r)
    outs = (m.x_in, out_hbm, m.out_s, m.out_r)
    gis = (m.cot_in, gi_hbm, m.gi_s, m.gi_r)

    gather_start(*ins, 0, 0)
    loads = [
        pltpu.make_async_copy(src, dst, m.load.at[i])
        for i, (src, dst) in enumerate(
            ((wq_hbm, m.w_qkv), (wo_hbm, m.w_out), (wu_hbm, m.w_up), (wd_hbm, m.w_down))
        )
    ]
    for load in loads:
        load.start()

    def orders(rows, columns, earlier, same, position):
        row = lax.broadcasted_iota(jnp.int32, (rows, columns), 0)
        column = lax.broadcasted_iota(jnp.int32, (rows, columns), 1)
        own = jnp.where(earlier(row, column), position(column), FAR)
        return jnp.where(same(row, column), -FAR, own)

    def near(lowest):
        return orders(
            WINDOW,
            2 * WINDOW,
            lambda r, c: (c < r + WINDOW) & (c > r) & (c >= lowest),
            lambda r, c: c == r + WINDOW,
            lambda c: c,
        )

    m.near_order[0] = near(WINDOW)
    m.near_order[1] = near(0)
    far_rows = nblk * GROUP
    m.far_order[...] = orders(
        far_rows,
        far_rows,
        lambda r, c: (c < r) & (((r - c) & (GROUP - 1)) == 0),
        lambda r, c: c == r,
        lambda c: (c // GROUP) * WINDOW + (c & (GROUP - 1)),
    )
    m.sums[...] = jnp.zeros_like(m.sums)
    for load in loads:
        load.wait()
    roomy = nblk <= ROOMY
    for l in range(layers if roomy else 0):
        m.w_out_t[l] = m.w_out[l].T
        for c in range(3):
            part = slice(c * CHUNK, (c + 1) * CHUNK)
            m.w_qkv_t[l, part] = m.w_qkv[l, :, part].T
        for c in range(hidden // CHUNK):
            part = slice(c * CHUNK, (c + 1) * CHUNK)
            m.w_up_t[l, part] = m.w_up[l, :, part].T
            m.w_down_t[l, :, part] = m.w_down[l, part].T

    def rows_of(t):
        return pl.ds(t * TILE, TILE)

    def back_dot(x, name, l):
        if roomy:
            return dot(x, getattr(m, name + "_t")[l])
        return dot_nt(x, getattr(m, name)[l])

    def lanes_of(t):
        return pl.ds(pl.multiple_of(t * TILE * WINDOW, TILE * WINDOW), TILE * WINDOW)

    def cols(c):
        return slice(c * CHUNK, (c + 1) * CHUNK)

    def loop(count, body, unroll=1):
        unroll = min(unroll, count)

        def step(i, carry):
            for e in range(unroll):
                body(i * unroll + e)
            return carry

        lax.fori_loop(0, count // unroll, step, 0)

    def near_tiles(i):
        return [i * AT_ONCE * near_each + e for e in range(AT_ONCE * near_each)]

    def far_tiles(i):
        return [i * AT_ONCE + e for e in range(AT_ONCE)]

    def window(ref, b, part):
        return jnp.concatenate([ref[jnp.maximum(b - 1, 0), :, part], ref[b, :, part]], axis=0)

    def spread(i):
        return pl.ds(pl.multiple_of(i * GROUP, GROUP), GROUP)

    def strided(v):
        return v.astype(BF16).reshape(nblk, GROUP, HEAD)

    def halves_of(t):
        step = TILE if roomy else 2
        return [pl.ds(t * TILE + i, step) for i in range(0, TILE, step)]

    def parts_of(rows):
        each = WINDOW // PIECE
        return [
            (rows.start + i // each, slice(i % each * PIECE, (i % each + 1) * PIECE), slice(i * PIECE, (i + 1) * PIECE))
            for i in range(rows.size * each)
        ]

    def store_norm(l, which, b, r, x, normed, gain, bias):
        hat, inverse = normalize(x)
        k = 2 * l + which
        m.stats[b, r, k : k + 1] = inverse
        normed[l, b, r] = (hat * gain[l : l + 1] + bias[l : l + 1]).astype(BF16)

    def source(l, s, b, r):
        if l == 0:
            return m.x_in[s * nblk + b, r].astype(F32)
        return m.dx[b, r]

    def forward(l, s):
        length = lens[me * ns + s]

        def project(t):
            for b, r, _ in parts_of(rows_of(t)):
                store_norm(l, 0, b, r, source(l, s, b, r), m.a1, gain1, bias1)
            rows = rows_of(t)
            a = flat(m.a1[l, rows])
            if roomy:
                m.a1_t[l, :, lanes_of(t)] = a.T
            m.qkv[l, rows] = blocks(dot(a, m.w_qkv[l]).astype(BF16))

        here = m.qkv.at[l]

        def attend(i):
            scores = [
                dot_nt(here[b, :, Q_NEAR], window(here, b, K_NEAR)) for b in near_tiles(i)
            ] + [dot_nt(flat(here[:, spread(j), Q_FAR]), flat(here[:, spread(j), K_FAR])) for j in far_tiles(i)]
            rules = [
                (m.near_order.at[jnp.minimum(b, 1)], length - (b - 1) * WINDOW) for b in near_tiles(i)
            ] + [(m.far_order, length - j * GROUP) for j in far_tiles(i)]
            p = [weights_of(x, *rule, factor) for x, rule in zip(scores, rules)]
            for b, x in zip(near_tiles(i), p):
                m.near_p[l, b] = x
                result = dot(x, window(here, b, V_NEAR))
                m.heads[l, b, :, 0:HEAD] = result.astype(BF16)
            for j, x in zip(far_tiles(i), p[len(near_tiles(i)) :]):
                m.far_p[l, j] = x
                result = dot(x, flat(here[:, spread(j), V_FAR]))
                m.heads[l, :, spread(j), HEAD:] = strided(result)

        def mix(t):
            rows = rows_of(t)
            mixed = dot(flat(m.heads[l, rows]), m.w_out[l])
            for b, r, i in parts_of(rows_of(t)):
                y = source(l, s, b, r) + mixed[i]
                m.dx[b, r] = y
                store_norm(l, 1, b, r, y, m.a2, gain2, bias2)
            if roomy:
                m.a2_t[l, :, lanes_of(t)] = flat(m.a2[l, rows]).T
            for half in halves_of(t):
                h = dot(flat(m.a2[l, half]), m.w_up[l])
                for b, r, i in parts_of(half):
                    for c in range(hidden // CHUNK):
                        m.act[l, b, r, cols(c)], m.slope[l, b, r, cols(c)] = gelu_pair(h[i, cols(c)])
            fed = dot(flat(m.act[l, rows]), m.w_down[l])
            for b, r, i in parts_of(rows_of(t)):
                y = m.dx[b, r] + fed[i]
                if l == layers - 1:
                    m.x_in[s * nblk + b, r] = y.astype(BF16)
                else:
                    m.dx[b, r] = y

        loop(tiles, project)
        loop(groups // AT_ONCE, attend)
        loop(tiles, mix)

    def unnorm(l, which, b, r, grad, normed, gain, bias, over):
        hat = (normed[l, b, r].astype(F32) - bias[l : l + 1]) * over
        k = 2 * l + which
        back = norm_back(grad, hat, m.stats[b, r, k : k + 1], gain[l : l + 1])
        return back, row_sums(grad * hat), row_sums(grad)

    def add_sums(l, which, terms):
        for k in range(2):
            total = terms[0][k]
            for term in terms[1:]:
                total = total + term[k]
            m.sums[l, 2 * which + k] += total

    def back_feed(l, s):
        def body(t):
            rows = rows_of(t)
            source = m.cot_in.at[pl.ds(s * nblk, nblk)] if l == layers - 1 else m.dx
            for b, r, _ in parts_of(rows_of(t)):
                m.df[b, r] = source[b, r].astype(BF16)
            m.df_t[:, lanes_of(t)] = flat(m.df[rows]).T
            m.heads_t[:, lanes_of(t)] = flat(m.heads[l, rows]).T
            for half in halves_of(t):
                dg = back_dot(flat(m.df[half]), "w_down", l)
                for b, r, i in parts_of(half):
                    for c in range(hidden // CHUNK):
                        slope = m.slope[l, b, r, cols(c)].astype(F32)
                        m.slope[l, b, r, cols(c)] = (dg[i, cols(c)] * slope).astype(BF16)
            da = back_dot(flat(m.slope[l, rows]), "w_up", l)
            over = 1.0 / gain2[l : l + 1]
            terms = []
            for b, r, i in parts_of(rows_of(t)):
                back, *term = unnorm(l, 1, b, r, da[i], m.a2, gain2, bias2, over)
                terms.append(term)
                dy = source[b, r].astype(F32) + back
                m.dx[b, r] = dy
                m.dm[b, r] = dy.astype(BF16)
            add_sums(l, 1, terms)
            do = back_dot(flat(m.dm[rows]), "w_out", l)
            m.do[pl.ds(t * TILE, TILE)] = blocks(do.astype(BF16))

        loop(tiles, body)

    def back_scores(p, dp):
        parts = []
        for r in pieces_of(dp.shape[0]):
            high = p[r].astype(F32)
            inner = jnp.sum(dp[r] * high, axis=1, keepdims=True)
            parts.append((high * (dp[r] - inner)).astype(BF16))
        return jnp.concatenate(parts, axis=0)

    def back_attend(l, s):
        here = m.qkv.at[l]
        near_p = m.near_p.at[l]

        def body(i):
            near, far = near_tiles(i), far_tiles(i)
            far_do = [flat(m.do[:, spread(j), HEAD:]) for j in far]
            far_p = [m.far_p[l, j] for j in far]
            dp = [dot_nt(m.do[b, :, 0:HEAD], window(here, b, V_NEAR)) for b in near]
            dp += [dot_nt(x, flat(here[:, spread(j), V_FAR])) for j, x in zip(far, far_do)]
            p = [near_p[b] for b in near] + far_p
            ds = [back_scores(x, y) for x, y in zip(p, dp)]
            for b, x in zip(near, ds):
                m.near_ds[b] = x
                m.near_dq[b] = (dot(x, window(here, b, K_NEAR)) * scale).astype(BF16)
            for j, do, w, x in zip(far, far_do, far_p, ds[len(near) :]):
                q = flat(here[:, spread(j), Q_FAR])
                dq = dot(x, flat(here[:, spread(j), K_FAR])) * scale
                dk = dot_tn(x, q) * scale
                dv = dot_tn(w, do)
                here[:, spread(j), Q_FAR] = strided(dq)
                here[:, spread(j), K_FAR] = strided(dk)
                here[:, spread(j), V_FAR] = strided(dv)

        loop(groups // AT_ONCE, body)
        for b in range(nblk):
            if b + 1 < nblk:
                both = slice(b, b + 2)
                ds = jnp.concatenate([m.near_ds[b, :, WINDOW:], m.near_ds[b + 1, :, :WINDOW]], axis=0)
                p = jnp.concatenate([near_p[b, :, WINDOW:], near_p[b + 1, :, :WINDOW]], axis=0)
                q, do = flat(here[both, :, Q_NEAR]), flat(m.do[both, :, 0:HEAD])
            else:
                ds, p = m.near_ds[b, :, WINDOW:], near_p[b, :, WINDOW:]
                q, do = here[b, :, Q_NEAR], m.do[b, :, 0:HEAD]
            here[b, :, K_NEAR] = (dot_tn(ds, q) * scale).astype(BF16)
            here[b, :, V_NEAR] = dot_tn(p, do).astype(BF16)
            here[b, :, Q_NEAR] = m.near_dq[b]

    def back_project(l, s):
        def body(t):
            da = back_dot(flat(m.qkv[l, rows_of(t)]), "w_qkv", l)
            over = 1.0 / gain1[l : l + 1]
            terms = []
            for b, r, i in parts_of(rows_of(t)):
                back, *term = unnorm(l, 0, b, r, da[i], m.a1, gain1, bias1, over)
                terms.append(term)
                if l == 0:
                    m.cot_in[s * nblk + b, r] = (m.dx[b, r] + back).astype(BF16)
                else:
                    m.dx[b, r] = m.dx[b, r] + back
            add_sums(l, 0, terms)

        loop(tiles, body)

    def outer(l, s, left, ref, first, flipped=False):
        if len(left.shape) == 2:
            product = dot(left[...], flat(ref[...]))
        else:
            product = dot_tn(flat(left[...]), flat(ref[...]))
        for c in range(product.shape[1] // CHUNK):
            part = product[:, cols(c)]
            part = part.T if flipped else part
            if s > 0:
                part = part + m.grad[l, cols(first + c)]
            m.grad[l, cols(first + c)] = part

    def grads_feed(l, s):
        outer(l, s, (m.a2_t if roomy else m.a2).at[l], m.slope.at[l], 0)
        outer(l, s, m.df_t, m.act.at[l], hidden // CHUNK, True)

    def grads_attend(l, s):
        first = 2 * hidden // CHUNK
        outer(l, s, m.heads_t, m.dm, first)
        outer(l, s, (m.a1_t if roomy else m.a1).at[l], m.qkv.at[l], first + 1)

    core = lax.rem(me, 2)
    second = lax.rem(me // 2, 2)
    bits = nw.bit_length() - 1

    def toggled(bit):
        size = 2**bit
        return me + size - 2 * size * lax.rem(me // size, 2)

    def reduction(l, which):
        start, count = ((0, 2 * hidden), (2 * hidden, 4 * CHUNK))[which]
        half, chunk, piece = count // 2, count // 2 // nb, count // 4 // nb
        lead = start // 2
        final = m.final.at[l]

        def span(at, size):
            return pl.ds(pl.multiple_of(at, 16), size)

        mine = start + core * half
        theirs = start + (1 - core) * half
        chunk_at = mine + mb * chunk
        piece_at = chunk_at + second * piece
        other_piece = chunk_at + (1 - second) * piece
        core_in = m.got_core.at[l, pl.ds(lead, half)]

        def remote(src, dst, name, k_send, k_recv, device):
            return pltpu.make_async_remote_copy(
                src_ref=src,
                dst_ref=dst,
                send_sem=getattr(m, name + "_s").at[l, which, k_send],
                recv_sem=getattr(m, name + "_r").at[l, which, k_recv],
                device_id=device,
                device_id_type=MESH,
            )

        def here(at, size):
            return final.at[span(at, size)]

        to_core = remote(m.put_core.at[pl.ds(0, half)], core_in, "core", 0, 0, (mb, toggled(0)))
        to_pair = remote(
            m.put_pair.at[pl.ds(start // 4 // nb, piece)],
            m.got_pair.at[l, pl.ds(start // 4 // nb, piece)],
            "pair", 0, 0, (mb, toggled(1)),
        )

        def to_batch(other, owner):
            return remote(
                m.put_batch.at[span(other * chunk, chunk)],
                m.got_batch.at[l, owner, pl.ds(start // 2 // nb, chunk)],
                "batch", other, owner, (other, me),
            )

        def to_top(bit):
            return remote(
                m.put_top.at[bit - 2, pl.ds(start // 4 // nb, piece)],
                m.got_top.at[l, bit - 2, pl.ds(start // 4 // nb, piece)],
                "top", bit - 2, bit - 2, (mb, toggled(bit)),
            )

        def pair_back(at):
            return remote(here(at, piece), here(at, piece), "pair_back", 0, 0, (mb, toggled(1)))

        def batch_back(other, owner):
            at = mine + owner * chunk
            return remote(here(at, chunk), here(at, chunk), "batch_back", other, owner, (other, me))

        def core_back(at):
            return remote(here(at, half), here(at, half), "core_back", 0, 0, (mb, toggled(0)))

        def others():
            return [lax.rem(mb + k, nb) for k in range(1, nb)]

        def step0():
            m.put_core[pl.ds(0, half)] = m.grad[l, span(theirs, half)].astype(BF16)
            to_core.start()

        def step1():
            to_core.wait()
            total = m.grad[l, span(mine, half)] + m.got_core[l, pl.ds(lead, half)].astype(F32)
            m.grad[l, span(mine, half)] = total
            m.put_batch[pl.ds(0, half)] = total.astype(BF16)
            for other in others():
                to_batch(other, mb).start()

        def step2():
            total = m.grad[l, span(chunk_at, chunk)]
            for other in others():
                to_batch(other, mb).wait_send()
                to_batch(other, other).wait_recv()
                got = m.got_batch[l, other, pl.ds(start // 2 // nb, chunk)]
                total = total + got.astype(F32)
            m.grad[l, span(chunk_at, chunk)] = total
            send = m.grad[l, span(other_piece, piece)]
            m.put_pair[pl.ds(start // 4 // nb, piece)] = send.astype(BF16)
            to_pair.start()

        def step3():
            to_pair.wait()
            got = m.got_pair[l, pl.ds(start // 4 // nb, piece)]
            total = m.grad[l, span(piece_at, piece)] + got.astype(F32)
            m.put_top[0, pl.ds(start // 4 // nb, piece)] = total.astype(BF16)
            to_top(2).start()

        def step4(bit=2):
            to_top(bit).wait()
            at = pl.ds(start // 4 // nb, piece)
            total = m.put_top[bit - 2, at].astype(F32) + m.got_top[l, bit - 2, at].astype(F32)
            if bit + 1 < bits:
                m.put_top[bit - 1, at] = total.astype(BF16)
                to_top(bit + 1).start()
                step4(bit + 1)
            else:
                final[span(piece_at, piece)] = total.astype(BF16)
                pair_back(piece_at).start()

        def step5():
            pair_back(other_piece).wait_recv()
            for other in others():
                batch_back(other, mb).start()

        def step6():
            for other in others():
                batch_back(other, other).wait_recv()
            core_back(mine).start()

        save = pltpu.make_async_copy(
            final.at[pl.ds(start, count)],
            grads_hbm.at[l, pl.ds(start, count)],
            m.save.at[l, which],
        )

        def step7():
            core_back(theirs).wait_recv()
            save.start()

        def step8():
            pair_back(piece_at).wait_send()
            for other in others():
                batch_back(other, mb).wait_send()
            core_back(mine).wait_send()
            save.wait()

        return [step0, step1, step2, step3, step4, step5, step6, step7, step8]

    sums = {(l, w): reduction(l, w) for l in range(layers) for w in range(2)}
    waiting = []

    def advance():
        for steps in list(waiting):
            steps.pop(0)()
            if not steps:
                waiting.remove(steps)

    def begin(l, which, last):
        if last:
            steps = sums[l, which]
            steps.pop(0)()
            waiting.append(steps)

    for s in range(ns):
        last = s == ns - 1
        gather_wait(*ins, 0, s)
        if s == 0:
            gather_start(*cots, 1, s)
        for l in range(layers):
            with jax.named_scope("layer_forward"):
                forward(l, s)
        gather_wait(*cots, 1, s)
        if not last:
            gather_start(*ins, 0, s + 1)
        else:
            scatter_start(*outs, 2, s)
        for l in reversed(range(layers)):
            with jax.named_scope("feed_backward"):
                back_feed(l, s)
            if l < layers - 1:
                advance()
            with jax.named_scope("feed_gradients"):
                grads_feed(l, s)
            begin(l, 0, last)
            with jax.named_scope("attention_backward"):
                back_attend(l, s)
            advance()
            if not last:
                if l == layers - 1:
                    gather_start(*cots, 1, s + 1)
                if l == 0:
                    scatter_start(*outs, 2, s)
            with jax.named_scope("attention_gradients"):
                grads_attend(l, s)
            begin(l, 1, last)
            with jax.named_scope("input_backward"):
                back_project(l, s)
            if l == 0:
                advance()
        scatter_start(*gis, 3, s)

    def norm_copy(own, slots, k, device, name, owner):
        return pltpu.make_async_remote_copy(
            src_ref=slots.at[own],
            dst_ref=slots.at[owner],
            send_sem=getattr(m, name + "_s").at[k],
            recv_sem=getattr(m, name + "_r").at[owner],
            device_id=device,
            device_id_type=MESH,
        )

    m.norm_all[me] = jnp.sum(m.sums[...].reshape(4 * layers, 8, width), axis=1)
    for k in range(1, nw):
        other = lax.rem(me + k, nw)
        norm_copy(me, m.norm_all, other, (mb, other), "norm_all", me).start()
    advance()
    for k in range(1, nw):
        other = lax.rem(me + k, nw)
        norm_copy(me, m.norm_all, other, (mb, other), "norm_all", other).wait_recv()
    total = m.norm_all[0]
    for k in range(1, nw):
        total = total + m.norm_all[k]
    m.norm_batch[mb] = total
    for k in range(1, nb):
        other = lax.rem(mb + k, nb)
        norm_copy(mb, m.norm_batch, other, (other, me), "norm_batch", mb).start()
    while waiting:
        advance()
    for k in range(1, nb):
        other = lax.rem(mb + k, nb)
        norm_copy(mb, m.norm_batch, other, (other, me), "norm_batch", other).wait_recv()
    total = m.norm_batch[0]
    for k in range(1, nb):
        total = total + m.norm_batch[k]
    norm_out[...] = total

    for k in range(1, nw):
        other = lax.rem(me + k, nw)
        norm_copy(me, m.norm_all, other, (mb, other), "norm_all", me).wait_send()
    for k in range(1, nb):
        other = lax.rem(mb + k, nb)
        norm_copy(mb, m.norm_batch, other, (other, me), "norm_batch", mb).wait_send()
    for s in range(ns):
        gather_end(*ins, s)
        gather_end(*cots, s)
        scatter_end(*outs, 2, s)
        scatter_end(*gis, 3, s)


def per_device(nb, nw, inputs, lengths, gain1, bias1, w_qkv, w_out, gain2, bias2, w_up, w_down, cotangent):
    count, block, width = inputs.shape
    layers, _, hidden = w_up.shape
    ns, per = count // nw, block // WINDOW
    pieces = plan(nb, nw, ns, nw * per, width, hidden, layers)
    shape = (nw, ns, per, WINDOW, width)
    anywhere = pl.BlockSpec(memory_space=pl.ANY)
    vmem = pl.BlockSpec(memory_space=pltpu.VMEM)
    rows = 12 * CHUNK

    def body(*refs):
        kernel(nb, nw, ns, list(pieces), *refs)

    outputs, grad_rows, grads, norms = pl.pallas_call(
        body,
        out_shape=(
            jax.ShapeDtypeStruct(shape, BF16),
            jax.ShapeDtypeStruct(shape, BF16),
            jax.ShapeDtypeStruct((layers, rows, CHUNK), BF16),
            jax.ShapeDtypeStruct((4 * layers, width), F32),
        ),
        in_specs=[pl.BlockSpec(memory_space=pltpu.SMEM)] + [anywhere] * 2 + [vmem] * 4 + [anywhere] * 4,
        out_specs=(anywhere, anywhere, anywhere, vmem),
        scratch_shapes=list(pieces.values()),
        compiler_params=pltpu.CompilerParams(
            collective_id=0, has_side_effects=True, vmem_limit_bytes=64 * 1024 * 1024
        ),
    )(
        lengths, inputs.reshape(shape), cotangent.reshape(shape),
        gain1, bias1, gain2, bias2, w_qkv, w_out, w_up, w_down,
    )
    each = hidden // CHUNK
    tokens = count * block // layers

    def finish(out_in, rows_in, grads_in, norm_in, *results):
        out_out, rows_out, qkv_out, rest_out, up_out, down_out, *norm_outs = results
        out_out[...] = out_in[...]
        rows_out[...] = rows_in[...].astype(F32)

        def part(c):
            return grads_in[0, c * CHUNK : (c + 1) * CHUNK].astype(F32)

        for c in range(each):
            up_out[0, :, c * CHUNK : (c + 1) * CHUNK] = part(c)
            down_out[0, c * CHUNK : (c + 1) * CHUNK] = part(each + c)
        rest_out[0] = part(2 * each)
        for c in range(3):
            qkv_out[0, :, c * CHUNK : (c + 1) * CHUNK] = part(2 * each + 1 + c)
        for l in range(layers):
            for k in range(4):
                norm_outs[k][l : l + 1] = norm_in[4 * l + k : 4 * l + k + 1]

    row_spec = pl.BlockSpec((tokens, width), lambda i: (i, 0))
    norm_spec = pl.BlockSpec((layers, width), lambda i: (0, 0))

    def layer_spec(*dims):
        return pl.BlockSpec((1, *dims), lambda i: (i, 0, 0))

    outputs, grad_rows, grad_qkv, grad_out, grad_up, grad_down, *norms = pl.pallas_call(
        finish,
        grid=(layers,),
        out_shape=(
            jax.ShapeDtypeStruct((count * block, width), BF16),
            jax.ShapeDtypeStruct((count * block, width), F32),
            jax.ShapeDtypeStruct((layers, width, 3 * width), F32),
            jax.ShapeDtypeStruct((layers, width, width), F32),
            jax.ShapeDtypeStruct((layers, width, hidden), F32),
            jax.ShapeDtypeStruct((layers, hidden, width), F32),
        )
        + (jax.ShapeDtypeStruct((layers, width), F32),) * 4,
        in_specs=[
            row_spec,
            row_spec,
            layer_spec(rows, CHUNK),
            pl.BlockSpec((4 * layers, width), lambda i: (0, 0)),
        ],
        out_specs=(
            row_spec,
            row_spec,
            layer_spec(width, 3 * width),
            layer_spec(width, width),
            layer_spec(width, hidden),
            layer_spec(hidden, width),
        )
        + (norm_spec,) * 4,
        compiler_params=pltpu.CompilerParams(vmem_limit_bytes=60 * 1024 * 1024),
    )(outputs.reshape(count * block, width), grad_rows.reshape(count * block, width), grads, norms)
    return (
        outputs.reshape(count, block, width),
        grad_rows.reshape(count, block, width),
        norms[0],
        norms[1],
        grad_qkv,
        grad_out,
        norms[2],
        norms[3],
        grad_up,
        grad_down,
    )


def solution(mesh):
    nb, nw = mesh.shape["batch"], mesh.shape["wide"]

    def step(*args):
        return per_device(nb, nw, *args)

    rows = P("batch", "wide", None)
    return jax.shard_map(
        step,
        mesh=mesh,
        in_specs=(rows, P("batch")) + (P(),) * 8 + (rows,),
        out_specs=(rows, rows) + (P(),) * 8,
        check_vma=False,
    )
```

```python
import types

import jax
import jax.numpy as jnp
from jax import lax
from jax.experimental import pallas as pl
from jax.experimental.pallas import tpu as pltpu
from jax.sharding import PartitionSpec as P

MESH = pl.DeviceIdType.MESH
F32, BF16 = jnp.float32, jnp.bfloat16
HEAD = 128
WINDOW = 128
GROUP = 16
TILE = 4
PIECE = 32
CHUNK = 256
ROOMY = 8
AT_ONCE = 4
Q_NEAR, Q_FAR, K_NEAR, K_FAR, V_NEAR, V_FAR = (slice(i * HEAD, (i + 1) * HEAD) for i in range(6))
FAR = 1 << 20
MASKED = -1e30
LOG2E = 1.4426950408889634
GELU_A = 0.7978845608028654
GELU_B = GELU_A * 0.044715


def dot(a, b):
    return lax.dot_general(a, b, (((1,), (0,)), ((), ())), preferred_element_type=F32)


def dot_nt(a, b):
    return lax.dot_general(a, b, (((1,), (1,)), ((), ())), preferred_element_type=F32)


def dot_tn(a, b):
    return lax.dot_general(a, b, (((0,), (0,)), ((), ())), preferred_element_type=F32)


def flat(v):
    return v.reshape(-1, v.shape[-1])


def blocks(v):
    return v.reshape(-1, WINDOW, v.shape[-1])


def normalize(x):
    center = x - jnp.mean(x, axis=-1, keepdims=True)
    inverse = lax.rsqrt(jnp.mean(center * center, axis=-1, keepdims=True) + 1e-05)
    return center * inverse, inverse


def norm_back(grad, hat, inverse, gain):
    scaled = grad * gain
    first = jnp.mean(scaled, axis=-1, keepdims=True)
    second = jnp.mean(scaled * hat, axis=-1, keepdims=True)
    return inverse * (scaled - first - hat * second)


def row_sums(v):
    return jnp.sum(v.reshape(-1, 8, v.shape[-1]), axis=0)


def pieces_of(rows):
    return [slice(i, i + PIECE) for i in range(0, rows, PIECE)]


def weights_of(scores, order, limit, factor):
    parts = []
    for r in pieces_of(scores.shape[0]):
        masked = jnp.where(order[r] < limit, scores[r], MASKED)
        peak = jnp.max(masked, axis=1, keepdims=True)
        powered = jnp.exp2((masked - peak) * factor)
        parts.append((powered * (1.0 / jnp.sum(powered, axis=1, keepdims=True))).astype(BF16))
    return jnp.concatenate(parts, axis=0)


def gelu_pair(h):
    square = h * h
    q = 0.5 * jnp.tanh(h * (GELU_B * square + GELU_A)) + 0.5
    g = h * q
    slope = q + g * (1.0 - q) * (6.0 * GELU_B * square + 2.0 * GELU_A)
    return g.astype(BF16), slope.astype(BF16)


def plan(nb, nw, ns, nblk, width, hidden, layers):
    total = ns * nblk
    far_rows = nblk * GROUP
    rows = 12 * CHUNK
    pieces = {}

    def vmem(name, dims, kind):
        pieces[name] = pltpu.VMEM(dims, kind)

    def sems(name, *dims):
        pieces[name] = pltpu.SemaphoreType.DMA(dims)

    vmem("x_in", (total, WINDOW, width), BF16)
    vmem("cot_in", (total, WINDOW, width), BF16)
    vmem("w_qkv", (layers, width, 3 * width), BF16)
    vmem("w_out", (layers, width, width), BF16)
    vmem("w_up", (layers, width, hidden), BF16)
    vmem("w_down", (layers, hidden, width), BF16)
    vmem("a1", (layers, nblk, WINDOW, width), BF16)
    vmem("a2", (layers, nblk, WINDOW, width), BF16)
    vmem("qkv", (layers, nblk, WINDOW, 3 * width), BF16)
    vmem("heads", (layers, nblk, WINDOW, width), BF16)
    vmem("near_p", (layers, nblk, WINDOW, 2 * WINDOW), BF16)
    vmem("far_p", (layers, WINDOW // GROUP, far_rows, far_rows), BF16)
    vmem("act", (layers, nblk, WINDOW, hidden), BF16)
    vmem("slope", (layers, nblk, WINDOW, hidden), BF16)
    vmem("stats", (nblk, WINDOW, WINDOW), F32)
    vmem("dx", (nblk, WINDOW, width), F32)
    vmem("df", (nblk, WINDOW, width), BF16)
    vmem("dm", (nblk, WINDOW, width), BF16)
    vmem("do", (nblk, WINDOW, width), BF16)
    vmem("near_ds", (nblk, WINDOW, 2 * WINDOW), BF16)
    vmem("near_dq", (nblk, WINDOW, HEAD), BF16)
    vmem("df_t", (width, nblk * WINDOW), BF16)
    vmem("heads_t", (width, nblk * WINDOW), BF16)
    if nblk <= ROOMY:
        vmem("a1_t", (layers, width, nblk * WINDOW), BF16)
        vmem("a2_t", (layers, width, nblk * WINDOW), BF16)
        vmem("w_qkv_t", (layers, 3 * width, width), BF16)
        vmem("w_out_t", (layers, width, width), BF16)
        vmem("w_up_t", (layers, hidden, width), BF16)
        vmem("w_down_t", (layers, width, hidden), BF16)
    vmem("near_order", (2, WINDOW, 2 * WINDOW), jnp.int32)
    vmem("far_order", (far_rows, far_rows), jnp.int32)
    vmem("sums", (layers, 4, 8, width), F32)
    vmem("grad", (layers, rows, CHUNK), F32)
    vmem("final", (layers, rows, CHUNK), BF16)
    vmem("got_core", (layers, rows // 2, CHUNK), BF16)
    vmem("got_batch", (layers, nb, rows // 2 // nb, CHUNK), BF16)
    vmem("got_pair", (layers, rows // 4 // nb, CHUNK), BF16)
    top = max(nw.bit_length() - 3, 1)
    vmem("got_top", (layers, top, rows // 4 // nb, CHUNK), BF16)
    vmem("put_core", (hidden + CHUNK // 2, CHUNK), BF16)
    vmem("put_batch", (hidden + CHUNK // 2, CHUNK), BF16)
    vmem("put_pair", (rows // 4 // nb, CHUNK), BF16)
    vmem("put_top", (top, rows // 4 // nb, CHUNK), BF16)
    vmem("norm_all", (nw, 4 * layers, width), F32)
    vmem("norm_batch", (nb, 4 * layers, width), F32)
    for name in ("in", "cot", "out", "gi"):
        sems(name + "_s", ns, nw)
        sems(name + "_r", ns, nw)
    sems("own", 4, ns)
    sems("load", 4)
    sems("save", layers, 2)
    for name, count in (("core", 1), ("batch", nb), ("pair", 1), ("top", top), ("pair_back", 1), ("batch_back", nb), ("core_back", 1)):
        sems(name + "_s", layers, 2, count)
        sems(name + "_r", layers, 2, count)
    sems("norm_all_s", nw)
    sems("norm_all_r", nw)
    sems("norm_batch_s", nb)
    sems("norm_batch_r", nb)
    return pieces


def kernel(nb, nw, ns, names, *refs):
    (lens, x_hbm, cot_hbm, gain1, bias1, gain2, bias2, wq_hbm, wo_hbm, wu_hbm, wd_hbm,
     out_hbm, gi_hbm, grads_hbm, norm_out) = refs[:15]
    m = types.SimpleNamespace(**dict(zip(names, refs[15:])))
    layers, width = gain1.shape
    hidden = wu_hbm.shape[2]
    per = x_hbm.shape[2]
    nblk = nw * per
    tiles = nblk // TILE
    groups = WINDOW // GROUP
    near_each = nblk // groups
    scale = float(HEAD) ** (-0.5)
    factor = scale * LOG2E
    me = lax.axis_index("wide")
    mb = lax.axis_index("batch")

    barrier = pltpu.get_barrier_semaphore()
    for k in range(1, nw):
        pl.semaphore_signal(barrier, inc=1, device_id=(mb, lax.rem(me + k, nw)), device_id_type=MESH)
    for k in range(1, nb):
        pl.semaphore_signal(barrier, inc=1, device_id=(lax.rem(mb + k, nb), me), device_id_type=MESH)
    pl.semaphore_wait(barrier, nw + nb - 2)

    def partner(k):
        place = me
        for bit in range(nw.bit_length() - 1):
            size = 2**bit
            if k & size:
                place = place + size - 2 * size * lax.rem(me // size, 2)
        return place

    far = [nw // 2 + k for k in range(nw // 2)]
    close = [k for k in range(nw // 2 - 1, 0, -1)]
    turns = [turn for pair in zip(far, close) for turn in pair] + [far[-1]]

    def gather_copy(src, dst, send, recv, s, other, owner):
        return pltpu.make_async_remote_copy(
            src_ref=src.at[other, s],
            dst_ref=dst.at[pl.ds(s * nblk + owner * per, per)],
            send_sem=send.at[s, other],
            recv_sem=recv.at[s, owner],
            device_id=(mb, other),
            device_id_type=MESH,
        )

    def gather_own(src, dst, which, s):
        return pltpu.make_async_copy(
            src.at[me, s], dst.at[pl.ds(s * nblk + me * per, per)], m.own.at[which, s]
        )

    def gather_start(src, dst, send, recv, which, s):
        for k in turns:
            gather_copy(src, dst, send, recv, s, partner(k), me).start()
        gather_own(src, dst, which, s).start()

    def gather_wait(src, dst, send, recv, which, s, steps=None):
        for k in range(1, nw) if steps is None else steps:
            other = partner(k)
            gather_copy(src, dst, send, recv, s, other, other).wait_recv()
        if steps is None or steps is close:
            gather_own(src, dst, which, s).wait()

    def gather_end(src, dst, send, recv, s):
        for k in range(1, nw):
            gather_copy(src, dst, send, recv, s, partner(k), me).wait_send()

    def scatter_copy(src, dst, send, recv, s, other, owner):
        return pltpu.make_async_remote_copy(
            src_ref=src.at[pl.ds(s * nblk + other * per, per)],
            dst_ref=dst.at[owner, s],
            send_sem=send.at[s, other],
            recv_sem=recv.at[s, owner],
            device_id=(mb, other),
            device_id_type=MESH,
        )

    def scatter_own(src, dst, which, s):
        return pltpu.make_async_copy(
            src.at[pl.ds(s * nblk + me * per, per)], dst.at[me, s], m.own.at[which, s]
        )

    def scatter_start(src, dst, send, recv, which, s, steps=None):
        for k in turns if steps is None else steps:
            scatter_copy(src, dst, send, recv, s, partner(k), me).start()
        if steps is None or steps is close:
            scatter_own(src, dst, which, s).start()

    def scatter_end(src, dst, send, recv, which, s):
        for k in range(1, nw):
            scatter_copy(src, dst, send, recv, s, partner(k), me).wait_send()
        for k in range(1, nw):
            other = partner(k)
            scatter_copy(src, dst, send, recv, s, other, other).wait_recv()
        scatter_own(src, dst, which, s).wait()

    ins = (x_hbm, m.x_in, m.in_s, m.in_r)
    cots = (cot_hbm, m.cot_in, m.cot_s, m.cot_r)
    outs = (m.x_in, out_hbm, m.out_s, m.out_r)
    gis = (m.cot_in, gi_hbm, m.gi_s, m.gi_r)

    gather_start(*ins, 0, 0)
    loads = [
        pltpu.make_async_copy(src, dst, m.load.at[i])
        for i, (src, dst) in enumerate(
            ((wq_hbm, m.w_qkv), (wo_hbm, m.w_out), (wu_hbm, m.w_up), (wd_hbm, m.w_down))
        )
    ]
    for load in loads:
        load.start()

    def orders(rows, columns, earlier, same, position):
        row = lax.broadcasted_iota(jnp.int32, (rows, columns), 0)
        column = lax.broadcasted_iota(jnp.int32, (rows, columns), 1)
        own = jnp.where(earlier(row, column), position(column), FAR)
        return jnp.where(same(row, column), -FAR, own)

    def near(lowest):
        return orders(
            WINDOW,
            2 * WINDOW,
            lambda r, c: (c < r + WINDOW) & (c > r) & (c >= lowest),
            lambda r, c: c == r + WINDOW,
            lambda c: c,
        )

    m.near_order[0] = near(WINDOW)
    m.near_order[1] = near(0)
    far_rows = nblk * GROUP
    m.far_order[...] = orders(
        far_rows,
        far_rows,
        lambda r, c: (c < r) & (((r - c) & (GROUP - 1)) == 0),
        lambda r, c: c == r,
        lambda c: (c // GROUP) * WINDOW + (c & (GROUP - 1)),
    )
    m.sums[...] = jnp.zeros_like(m.sums)
    for load in loads:
        load.wait()
    roomy = nblk <= ROOMY
    for l in range(layers if roomy else 0):
        m.w_out_t[l] = m.w_out[l].T
        for c in range(3):
            part = slice(c * CHUNK, (c + 1) * CHUNK)
            m.w_qkv_t[l, part] = m.w_qkv[l, :, part].T
        for c in range(hidden // CHUNK):
            part = slice(c * CHUNK, (c + 1) * CHUNK)
            m.w_up_t[l, part] = m.w_up[l, :, part].T
            m.w_down_t[l, :, part] = m.w_down[l, part].T

    def rows_of(t):
        return pl.ds(t * TILE, TILE)

    def back_dot(x, name, l):
        if roomy:
            return dot(x, getattr(m, name + "_t")[l])
        return dot_nt(x, getattr(m, name)[l])

    def lanes_of(t):
        return pl.ds(pl.multiple_of(t * TILE * WINDOW, TILE * WINDOW), TILE * WINDOW)

    def cols(c):
        return slice(c * CHUNK, (c + 1) * CHUNK)

    def loop(count, body, unroll=1):
        unroll = min(unroll, count)

        def step(i, carry):
            for e in range(unroll):
                body(i * unroll + e)
            return carry

        lax.fori_loop(0, count // unroll, step, 0)

    def near_tiles(i):
        return [i * AT_ONCE * near_each + e for e in range(AT_ONCE * near_each)]

    def far_tiles(i):
        return [i * AT_ONCE + e for e in range(AT_ONCE)]

    def window(ref, b, part):
        return jnp.concatenate([ref[jnp.maximum(b - 1, 0), :, part], ref[b, :, part]], axis=0)

    def spread(i):
        return pl.ds(pl.multiple_of(i * GROUP, GROUP), GROUP)

    def strided(v):
        return v.astype(BF16).reshape(nblk, GROUP, HEAD)

    def halves_of(t):
        step = TILE if roomy else 2
        return [pl.ds(t * TILE + i, step) for i in range(0, TILE, step)]

    def parts_of(rows):
        each = WINDOW // PIECE
        return [
            (rows.start + i // each, slice(i % each * PIECE, (i % each + 1) * PIECE), slice(i * PIECE, (i + 1) * PIECE))
            for i in range(rows.size * each)
        ]

    def store_norm(l, which, b, r, x, normed, gain, bias):
        hat, inverse = normalize(x)
        k = 2 * l + which
        m.stats[b, r, k : k + 1] = inverse
        normed[l, b, r] = (hat * gain[l : l + 1] + bias[l : l + 1]).astype(BF16)

    def source(l, s, b, r):
        if l == 0:
            return m.x_in[s * nblk + b, r].astype(F32)
        return m.dx[b, r]

    def forward(l, s):
        length = lens[me * ns + s]

        def project(t):
            for b, r, _ in parts_of(rows_of(t)):
                store_norm(l, 0, b, r, source(l, s, b, r), m.a1, gain1, bias1)
            rows = rows_of(t)
            a = flat(m.a1[l, rows])
            if roomy:
                m.a1_t[l, :, lanes_of(t)] = a.T
            m.qkv[l, rows] = blocks(dot(a, m.w_qkv[l]).astype(BF16))

        here = m.qkv.at[l]

        def attend(i):
            scores = [
                dot_nt(here[b, :, Q_NEAR], window(here, b, K_NEAR)) for b in near_tiles(i)
            ] + [dot_nt(flat(here[:, spread(j), Q_FAR]), flat(here[:, spread(j), K_FAR])) for j in far_tiles(i)]
            rules = [
                (m.near_order.at[jnp.minimum(b, 1)], length - (b - 1) * WINDOW) for b in near_tiles(i)
            ] + [(m.far_order, length - j * GROUP) for j in far_tiles(i)]
            p = [weights_of(x, *rule, factor) for x, rule in zip(scores, rules)]
            for b, x in zip(near_tiles(i), p):
                m.near_p[l, b] = x
                result = dot(x, window(here, b, V_NEAR))
                m.heads[l, b, :, 0:HEAD] = result.astype(BF16)
            for j, x in zip(far_tiles(i), p[len(near_tiles(i)) :]):
                m.far_p[l, j] = x
                result = dot(x, flat(here[:, spread(j), V_FAR]))
                m.heads[l, :, spread(j), HEAD:] = strided(result)

        def mix(t):
            rows = rows_of(t)
            mixed = dot(flat(m.heads[l, rows]), m.w_out[l])
            for b, r, i in parts_of(rows_of(t)):
                y = source(l, s, b, r) + mixed[i]
                m.dx[b, r] = y
                store_norm(l, 1, b, r, y, m.a2, gain2, bias2)
            if roomy:
                m.a2_t[l, :, lanes_of(t)] = flat(m.a2[l, rows]).T
            for half in halves_of(t):
                h = dot(flat(m.a2[l, half]), m.w_up[l])
                for b, r, i in parts_of(half):
                    for c in range(hidden // CHUNK):
                        m.act[l, b, r, cols(c)], m.slope[l, b, r, cols(c)] = gelu_pair(h[i, cols(c)])
            fed = dot(flat(m.act[l, rows]), m.w_down[l])
            for b, r, i in parts_of(rows_of(t)):
                y = m.dx[b, r] + fed[i]
                if l == layers - 1:
                    m.x_in[s * nblk + b, r] = y.astype(BF16)
                else:
                    m.dx[b, r] = y

        loop(tiles, project)
        loop(groups // AT_ONCE, attend)
        loop(tiles, mix)

    def unnorm(l, which, b, r, grad, normed, gain, bias, over):
        hat = (normed[l, b, r].astype(F32) - bias[l : l + 1]) * over
        k = 2 * l + which
        back = norm_back(grad, hat, m.stats[b, r, k : k + 1], gain[l : l + 1])
        return back, row_sums(grad * hat), row_sums(grad)

    def add_sums(l, which, terms):
        for k in range(2):
            total = terms[0][k]
            for term in terms[1:]:
                total = total + term[k]
            m.sums[l, 2 * which + k] += total

    def back_feed(l, s):
        def body(t):
            rows = rows_of(t)
            source = m.cot_in.at[pl.ds(s * nblk, nblk)] if l == layers - 1 else m.dx
            for b, r, _ in parts_of(rows_of(t)):
                m.df[b, r] = source[b, r].astype(BF16)
            m.df_t[:, lanes_of(t)] = flat(m.df[rows]).T
            m.heads_t[:, lanes_of(t)] = flat(m.heads[l, rows]).T
            for half in halves_of(t):
                dg = back_dot(flat(m.df[half]), "w_down", l)
                for b, r, i in parts_of(half):
                    for c in range(hidden // CHUNK):
                        slope = m.slope[l, b, r, cols(c)].astype(F32)
                        m.slope[l, b, r, cols(c)] = (dg[i, cols(c)] * slope).astype(BF16)
            da = back_dot(flat(m.slope[l, rows]), "w_up", l)
            over = 1.0 / gain2[l : l + 1]
            terms = []
            for b, r, i in parts_of(rows_of(t)):
                back, *term = unnorm(l, 1, b, r, da[i], m.a2, gain2, bias2, over)
                terms.append(term)
                dy = source[b, r].astype(F32) + back
                m.dx[b, r] = dy
                m.dm[b, r] = dy.astype(BF16)
            add_sums(l, 1, terms)
            do = back_dot(flat(m.dm[rows]), "w_out", l)
            m.do[pl.ds(t * TILE, TILE)] = blocks(do.astype(BF16))

        loop(tiles, body)

    def back_scores(p, dp):
        parts = []
        for r in pieces_of(dp.shape[0]):
            high = p[r].astype(F32)
            inner = jnp.sum(dp[r] * high, axis=1, keepdims=True)
            parts.append((high * (dp[r] - inner)).astype(BF16))
        return jnp.concatenate(parts, axis=0)

    def back_attend(l, s):
        here = m.qkv.at[l]
        near_p = m.near_p.at[l]

        def body(i):
            near, far = near_tiles(i), far_tiles(i)
            far_do = [flat(m.do[:, spread(j), HEAD:]) for j in far]
            far_p = [m.far_p[l, j] for j in far]
            dp = [dot_nt(m.do[b, :, 0:HEAD], window(here, b, V_NEAR)) for b in near]
            dp += [dot_nt(x, flat(here[:, spread(j), V_FAR])) for j, x in zip(far, far_do)]
            p = [near_p[b] for b in near] + far_p
            ds = [back_scores(x, y) for x, y in zip(p, dp)]
            for b, x in zip(near, ds):
                m.near_ds[b] = x
                m.near_dq[b] = (dot(x, window(here, b, K_NEAR)) * scale).astype(BF16)
            for j, do, w, x in zip(far, far_do, far_p, ds[len(near) :]):
                q = flat(here[:, spread(j), Q_FAR])
                dq = dot(x, flat(here[:, spread(j), K_FAR])) * scale
                dk = dot_tn(x, q) * scale
                dv = dot_tn(w, do)
                here[:, spread(j), Q_FAR] = strided(dq)
                here[:, spread(j), K_FAR] = strided(dk)
                here[:, spread(j), V_FAR] = strided(dv)

        loop(groups // AT_ONCE, body)
        for b in range(nblk):
            if b + 1 < nblk:
                both = slice(b, b + 2)
                ds = jnp.concatenate([m.near_ds[b, :, WINDOW:], m.near_ds[b + 1, :, :WINDOW]], axis=0)
                p = jnp.concatenate([near_p[b, :, WINDOW:], near_p[b + 1, :, :WINDOW]], axis=0)
                q, do = flat(here[both, :, Q_NEAR]), flat(m.do[both, :, 0:HEAD])
            else:
                ds, p = m.near_ds[b, :, WINDOW:], near_p[b, :, WINDOW:]
                q, do = here[b, :, Q_NEAR], m.do[b, :, 0:HEAD]
            here[b, :, K_NEAR] = (dot_tn(ds, q) * scale).astype(BF16)
            here[b, :, V_NEAR] = dot_tn(p, do).astype(BF16)
            here[b, :, Q_NEAR] = m.near_dq[b]

    def back_project(l, s):
        def body(t):
            da = back_dot(flat(m.qkv[l, rows_of(t)]), "w_qkv", l)
            over = 1.0 / gain1[l : l + 1]
            terms = []
            for b, r, i in parts_of(rows_of(t)):
                back, *term = unnorm(l, 0, b, r, da[i], m.a1, gain1, bias1, over)
                terms.append(term)
                if l == 0:
                    m.cot_in[s * nblk + b, r] = (m.dx[b, r] + back).astype(BF16)
                else:
                    m.dx[b, r] = m.dx[b, r] + back
            add_sums(l, 0, terms)

        loop(tiles, body)

    def outer(l, s, left, ref, first, flipped=False):
        if len(left.shape) == 2:
            product = dot(left[...], flat(ref[...]))
        else:
            product = dot_tn(flat(left[...]), flat(ref[...]))
        for c in range(product.shape[1] // CHUNK):
            part = product[:, cols(c)]
            part = part.T if flipped else part
            if s > 0:
                part = part + m.grad[l, cols(first + c)]
            m.grad[l, cols(first + c)] = part

    def grads_feed(l, s):
        outer(l, s, (m.a2_t if roomy else m.a2).at[l], m.slope.at[l], 0)
        outer(l, s, m.df_t, m.act.at[l], hidden // CHUNK, True)
        outer(l, s, m.heads_t, m.dm, 2 * hidden // CHUNK)

    def grads_attend(l, s):
        outer(l, s, (m.a1_t if roomy else m.a1).at[l], m.qkv.at[l], 2 * hidden // CHUNK + 1)

    core = lax.rem(me, 2)
    second = lax.rem(me // 2, 2)
    bits = nw.bit_length() - 1

    def toggled(bit):
        size = 2**bit
        return me + size - 2 * size * lax.rem(me // size, 2)

    split = 2 * hidden + (CHUNK if CHUNK % (64 * nb) == 0 else 0)

    def reduction(l, which):
        start, count = ((0, split), (split, 12 * CHUNK - split))[which]
        half, chunk, piece = count // 2, count // 2 // nb, count // 4 // nb
        lead = start // 2
        final = m.final.at[l]

        def span(at, size):
            return pl.ds(pl.multiple_of(at, 16), size)

        mine = start + core * half
        theirs = start + (1 - core) * half
        chunk_at = mine + mb * chunk
        piece_at = chunk_at + second * piece
        other_piece = chunk_at + (1 - second) * piece
        core_in = m.got_core.at[l, pl.ds(lead, half)]

        def remote(src, dst, name, k_send, k_recv, device):
            return pltpu.make_async_remote_copy(
                src_ref=src,
                dst_ref=dst,
                send_sem=getattr(m, name + "_s").at[l, which, k_send],
                recv_sem=getattr(m, name + "_r").at[l, which, k_recv],
                device_id=device,
                device_id_type=MESH,
            )

        def here(at, size):
            return final.at[span(at, size)]

        to_core = remote(m.put_core.at[pl.ds(0, half)], core_in, "core", 0, 0, (mb, toggled(0)))
        to_pair = remote(
            m.put_pair.at[pl.ds(start // 4 // nb, piece)],
            m.got_pair.at[l, pl.ds(start // 4 // nb, piece)],
            "pair", 0, 0, (mb, toggled(1)),
        )

        def to_batch(other, owner):
            return remote(
                m.put_batch.at[span(other * chunk, chunk)],
                m.got_batch.at[l, owner, pl.ds(start // 2 // nb, chunk)],
                "batch", other, owner, (other, me),
            )

        def to_top(bit):
            return remote(
                m.put_top.at[bit - 2, pl.ds(start // 4 // nb, piece)],
                m.got_top.at[l, bit - 2, pl.ds(start // 4 // nb, piece)],
                "top", bit - 2, bit - 2, (mb, toggled(bit)),
            )

        def pair_back(at):
            return remote(here(at, piece), here(at, piece), "pair_back", 0, 0, (mb, toggled(1)))

        def batch_back(other, owner):
            at = mine + owner * chunk
            return remote(here(at, chunk), here(at, chunk), "batch_back", other, owner, (other, me))

        def core_back(at):
            return remote(here(at, half), here(at, half), "core_back", 0, 0, (mb, toggled(0)))

        def others():
            return [lax.rem(mb + k, nb) for k in range(1, nb)]

        def step0():
            m.put_core[pl.ds(0, half)] = m.grad[l, span(theirs, half)].astype(BF16)
            to_core.start()

        def step1():
            to_core.wait()
            total = m.grad[l, span(mine, half)] + m.got_core[l, pl.ds(lead, half)].astype(F32)
            m.grad[l, span(mine, half)] = total
            m.put_batch[pl.ds(0, half)] = total.astype(BF16)
            for other in others():
                to_batch(other, mb).start()

        def step2():
            total = m.grad[l, span(chunk_at, chunk)]
            for other in others():
                to_batch(other, mb).wait_send()
                to_batch(other, other).wait_recv()
                got = m.got_batch[l, other, pl.ds(start // 2 // nb, chunk)]
                total = total + got.astype(F32)
            m.grad[l, span(chunk_at, chunk)] = total
            send = m.grad[l, span(other_piece, piece)]
            m.put_pair[pl.ds(start // 4 // nb, piece)] = send.astype(BF16)
            to_pair.start()

        def step3():
            to_pair.wait()
            got = m.got_pair[l, pl.ds(start // 4 // nb, piece)]
            total = m.grad[l, span(piece_at, piece)] + got.astype(F32)
            m.put_top[0, pl.ds(start // 4 // nb, piece)] = total.astype(BF16)
            to_top(2).start()

        def step4(bit=2):
            to_top(bit).wait()
            at = pl.ds(start // 4 // nb, piece)
            total = m.put_top[bit - 2, at].astype(F32) + m.got_top[l, bit - 2, at].astype(F32)
            if bit + 1 < bits:
                m.put_top[bit - 1, at] = total.astype(BF16)
                to_top(bit + 1).start()
                step4(bit + 1)
            else:
                final[span(piece_at, piece)] = total.astype(BF16)
                pair_back(piece_at).start()

        def step5():
            pair_back(other_piece).wait_recv()
            for other in others():
                batch_back(other, mb).start()

        def step6():
            for other in others():
                batch_back(other, other).wait_recv()
            core_back(mine).start()

        save = pltpu.make_async_copy(
            final.at[pl.ds(start, count)],
            grads_hbm.at[l, pl.ds(start, count)],
            m.save.at[l, which],
        )

        def step7():
            core_back(theirs).wait_recv()
            save.start()

        def step8():
            pair_back(piece_at).wait_send()
            for other in others():
                batch_back(other, mb).wait_send()
            core_back(mine).wait_send()
            save.wait()

        return [step0, step1, step2, step3, step4, step5, step6, step7, step8]

    sums = {(l, w): reduction(l, w) for l in range(layers) for w in range(2)}
    waiting = []

    def advance():
        for steps in list(waiting):
            steps.pop(0)()
            if not steps:
                waiting.remove(steps)

    def begin(l, which, last):
        if last:
            steps = sums[l, which]
            steps.pop(0)()
            waiting.append(steps)

    for s in range(ns):
        last = s == ns - 1
        gather_wait(*ins, 0, s, close)
        gather_wait(*ins, 0, s, far[: len(far) // 2])
        if s == 0:
            gather_start(*cots, 1, s)
        gather_wait(*ins, 0, s, far[len(far) // 2 :])
        for l in range(layers):
            with jax.named_scope("layer_forward"):
                forward(l, s)
        gather_wait(*cots, 1, s)
        if not last:
            gather_start(*ins, 0, s + 1)
        else:
            scatter_start(*outs, 2, s)
        for l in reversed(range(layers)):
            with jax.named_scope("feed_backward"):
                back_feed(l, s)
            if l < layers - 1:
                advance()
            with jax.named_scope("feed_gradients"):
                grads_feed(l, s)
            begin(l, 0, last)
            with jax.named_scope("attention_backward"):
                back_attend(l, s)
            advance()
            if not last:
                if l == layers - 1:
                    gather_start(*cots, 1, s + 1)
                if l == 0:
                    scatter_start(*outs, 2, s)
            with jax.named_scope("attention_gradients"):
                grads_attend(l, s)
            begin(l, 1, last)
            with jax.named_scope("input_backward"):
                back_project(l, s)
            if l == 0:
                advance()
        if not last:
            scatter_start(*gis, 3, s)
    scatter_start(*gis, 3, ns - 1, far[: len(far) // 2])
    scatter_start(*gis, 3, ns - 1, close)

    def norm_copy(own, slots, k, device, name, owner):
        return pltpu.make_async_remote_copy(
            src_ref=slots.at[own],
            dst_ref=slots.at[owner],
            send_sem=getattr(m, name + "_s").at[k],
            recv_sem=getattr(m, name + "_r").at[owner],
            device_id=device,
            device_id_type=MESH,
        )

    m.norm_all[me] = jnp.sum(m.sums[...].reshape(4 * layers, 8, width), axis=1)
    for k in range(1, nw):
        other = lax.rem(me + k, nw)
        norm_copy(me, m.norm_all, other, (mb, other), "norm_all", me).start()
    for _ in range(3):
        advance()
    scatter_start(*gis, 3, ns - 1, far[len(far) // 2 :])
    for k in range(1, nw):
        other = lax.rem(me + k, nw)
        norm_copy(me, m.norm_all, other, (mb, other), "norm_all", other).wait_recv()
    total = m.norm_all[0]
    for k in range(1, nw):
        total = total + m.norm_all[k]
    m.norm_batch[mb] = total
    for k in range(1, nb):
        other = lax.rem(mb + k, nb)
        norm_copy(mb, m.norm_batch, other, (other, me), "norm_batch", mb).start()
    while waiting:
        advance()
    for k in range(1, nb):
        other = lax.rem(mb + k, nb)
        norm_copy(mb, m.norm_batch, other, (other, me), "norm_batch", other).wait_recv()
    total = m.norm_batch[0]
    for k in range(1, nb):
        total = total + m.norm_batch[k]
    norm_out[...] = total

    for k in range(1, nw):
        other = lax.rem(me + k, nw)
        norm_copy(me, m.norm_all, other, (mb, other), "norm_all", me).wait_send()
    for k in range(1, nb):
        other = lax.rem(mb + k, nb)
        norm_copy(mb, m.norm_batch, other, (other, me), "norm_batch", mb).wait_send()
    for s in range(ns):
        gather_end(*ins, s)
        gather_end(*cots, s)
        scatter_end(*outs, 2, s)
        scatter_end(*gis, 3, s)


def per_device(nb, nw, inputs, lengths, gain1, bias1, w_qkv, w_out, gain2, bias2, w_up, w_down, cotangent):
    count, block, width = inputs.shape
    layers, _, hidden = w_up.shape
    ns, per = count // nw, block // WINDOW
    pieces = plan(nb, nw, ns, nw * per, width, hidden, layers)
    shape = (nw, ns, per, WINDOW, width)
    anywhere = pl.BlockSpec(memory_space=pl.ANY)
    vmem = pl.BlockSpec(memory_space=pltpu.VMEM)
    rows = 12 * CHUNK

    def body(*refs):
        kernel(nb, nw, ns, list(pieces), *refs)

    outputs, grad_rows, grads, norms = pl.pallas_call(
        body,
        out_shape=(
            jax.ShapeDtypeStruct(shape, BF16),
            jax.ShapeDtypeStruct(shape, BF16),
            jax.ShapeDtypeStruct((layers, rows, CHUNK), BF16),
            jax.ShapeDtypeStruct((4 * layers, width), F32),
        ),
        in_specs=[pl.BlockSpec(memory_space=pltpu.SMEM)] + [anywhere] * 2 + [vmem] * 4 + [anywhere] * 4,
        out_specs=(anywhere, anywhere, anywhere, vmem),
        scratch_shapes=list(pieces.values()),
        compiler_params=pltpu.CompilerParams(
            collective_id=0, has_side_effects=True, vmem_limit_bytes=64 * 1024 * 1024
        ),
    )(
        lengths, inputs.reshape(shape), cotangent.reshape(shape),
        gain1, bias1, gain2, bias2, w_qkv, w_out, w_up, w_down,
    )
    each = hidden // CHUNK
    tokens = count * block // layers

    def finish(out_in, rows_in, grads_in, norm_in, *results):
        out_out, rows_out, qkv_out, rest_out, up_out, down_out, *norm_outs = results
        out_out[...] = out_in[...]
        rows_out[...] = rows_in[...].astype(F32)

        def part(c):
            return grads_in[0, c * CHUNK : (c + 1) * CHUNK].astype(F32)

        for c in range(each):
            up_out[0, :, c * CHUNK : (c + 1) * CHUNK] = part(c)
            down_out[0, c * CHUNK : (c + 1) * CHUNK] = part(each + c)
        rest_out[0] = part(2 * each)
        for c in range(3):
            qkv_out[0, :, c * CHUNK : (c + 1) * CHUNK] = part(2 * each + 1 + c)
        for l in range(layers):
            for k in range(4):
                norm_outs[k][l : l + 1] = norm_in[4 * l + k : 4 * l + k + 1]

    row_spec = pl.BlockSpec((tokens, width), lambda i: (i, 0))
    norm_spec = pl.BlockSpec((layers, width), lambda i: (0, 0))

    def layer_spec(*dims):
        return pl.BlockSpec((1, *dims), lambda i: (i, 0, 0))

    outputs, grad_rows, grad_qkv, grad_out, grad_up, grad_down, *norms = pl.pallas_call(
        finish,
        grid=(layers,),
        out_shape=(
            jax.ShapeDtypeStruct((count * block, width), BF16),
            jax.ShapeDtypeStruct((count * block, width), F32),
            jax.ShapeDtypeStruct((layers, width, 3 * width), F32),
            jax.ShapeDtypeStruct((layers, width, width), F32),
            jax.ShapeDtypeStruct((layers, width, hidden), F32),
            jax.ShapeDtypeStruct((layers, hidden, width), F32),
        )
        + (jax.ShapeDtypeStruct((layers, width), F32),) * 4,
        in_specs=[
            row_spec,
            row_spec,
            layer_spec(rows, CHUNK),
            pl.BlockSpec((4 * layers, width), lambda i: (0, 0)),
        ],
        out_specs=(
            row_spec,
            row_spec,
            layer_spec(width, 3 * width),
            layer_spec(width, width),
            layer_spec(width, hidden),
            layer_spec(hidden, width),
        )
        + (norm_spec,) * 4,
        compiler_params=pltpu.CompilerParams(vmem_limit_bytes=60 * 1024 * 1024),
    )(outputs.reshape(count * block, width), grad_rows.reshape(count * block, width), grads, norms)
    return (
        outputs.reshape(count, block, width),
        grad_rows.reshape(count, block, width),
        norms[0],
        norms[1],
        grad_qkv,
        grad_out,
        norms[2],
        norms[3],
        grad_up,
        grad_down,
    )


def solution(mesh):
    nb, nw = mesh.shape["batch"], mesh.shape["wide"]

    def step(*args):
        return per_device(nb, nw, *args)

    rows = P("batch", "wide", None)
    return jax.shard_map(
        step,
        mesh=mesh,
        in_specs=(rows, P("batch")) + (P(),) * 8 + (rows,),
        out_specs=(rows, rows) + (P(),) * 8,
        check_vma=False,
    )
```

```python
import types

import jax
import jax.numpy as jnp
from jax import lax
from jax.experimental import pallas as pl
from jax.experimental.pallas import tpu as pltpu
from jax.sharding import PartitionSpec as P

MESH = pl.DeviceIdType.MESH
F32, BF16 = jnp.float32, jnp.bfloat16
HEAD = 128
WINDOW = 128
GROUP = 16
TILE = 4
PIECE = 32
CHUNK = 256
ROOMY = 8
AT_ONCE = 4
Q_NEAR, Q_FAR, K_NEAR, K_FAR, V_NEAR, V_FAR = (slice(i * HEAD, (i + 1) * HEAD) for i in range(6))
FAR = 1 << 20
MASKED = -1e30
LOG2E = 1.4426950408889634
GELU_A = 0.7978845608028654
GELU_B = GELU_A * 0.044715


def dot(a, b):
    return lax.dot_general(a, b, (((1,), (0,)), ((), ())), preferred_element_type=F32)


def dot_nt(a, b):
    return lax.dot_general(a, b, (((1,), (1,)), ((), ())), preferred_element_type=F32)


def dot_tn(a, b):
    return lax.dot_general(a, b, (((0,), (0,)), ((), ())), preferred_element_type=F32)


def flat(v):
    return v.reshape(-1, v.shape[-1])


def blocks(v):
    return v.reshape(-1, WINDOW, v.shape[-1])


def normalize(x):
    center = x - jnp.mean(x, axis=-1, keepdims=True)
    inverse = lax.rsqrt(jnp.mean(center * center, axis=-1, keepdims=True) + 1e-05)
    return center * inverse, inverse


def norm_back(grad, hat, inverse, gain):
    scaled = grad * gain
    first = jnp.mean(scaled, axis=-1, keepdims=True)
    second = jnp.mean(scaled * hat, axis=-1, keepdims=True)
    return inverse * (scaled - first - hat * second)


def row_sums(v):
    return jnp.sum(v.reshape(-1, 8, v.shape[-1]), axis=0)


def pieces_of(rows):
    return [slice(i, i + PIECE) for i in range(0, rows, PIECE)]


def weights_of(scores, order, limit, factor):
    parts = []
    for r in pieces_of(scores.shape[0]):
        masked = jnp.where(order[r] < limit, scores[r], MASKED)
        peak = jnp.max(masked, axis=1, keepdims=True)
        powered = jnp.exp2((masked - peak) * factor)
        parts.append((powered * (1.0 / jnp.sum(powered, axis=1, keepdims=True))).astype(BF16))
    return jnp.concatenate(parts, axis=0)


def gelu_pair(h):
    square = h * h
    q = 0.5 * jnp.tanh(h * (GELU_B * square + GELU_A)) + 0.5
    g = h * q
    slope = q + g * (1.0 - q) * (6.0 * GELU_B * square + 2.0 * GELU_A)
    return g.astype(BF16), slope.astype(BF16)


def first_rows(nb, hidden):
    return 2 * hidden + (CHUNK if CHUNK % (64 * nb) == 0 else 0)


def plan(nb, nw, ns, nblk, width, hidden, layers):
    total = ns * nblk
    far_rows = nblk * GROUP
    rows = 12 * CHUNK
    pieces = {}

    def vmem(name, dims, kind):
        pieces[name] = pltpu.VMEM(dims, kind)

    def sems(name, *dims):
        pieces[name] = pltpu.SemaphoreType.DMA(dims)

    vmem("x_in", (total, WINDOW, width), BF16)
    vmem("cot_in", (total, WINDOW, width), BF16)
    vmem("w_qkv", (layers, width, 3 * width), BF16)
    vmem("w_out", (layers, width, width), BF16)
    vmem("w_up", (layers, width, hidden), BF16)
    vmem("w_down", (layers, hidden, width), BF16)
    vmem("a1", (layers, nblk, WINDOW, width), BF16)
    vmem("a2", (layers, nblk, WINDOW, width), BF16)
    vmem("qkv", (layers, nblk, WINDOW, 3 * width), BF16)
    vmem("heads", (layers, nblk, WINDOW, width), BF16)
    vmem("near_p", (layers, nblk, WINDOW, 2 * WINDOW), BF16)
    vmem("far_p", (layers, WINDOW // GROUP, far_rows, far_rows), BF16)
    vmem("act", (layers, nblk, WINDOW, hidden), BF16)
    vmem("slope", (layers, nblk, WINDOW, hidden), BF16)
    vmem("stats", (nblk, WINDOW, WINDOW), F32)
    vmem("dx", (nblk, WINDOW, width), F32)
    vmem("df", (nblk, WINDOW, width), BF16)
    vmem("dm", (nblk, WINDOW, width), BF16)
    vmem("do", (nblk, WINDOW, width), BF16)
    vmem("near_ds", (nblk, WINDOW, 2 * WINDOW), BF16)
    vmem("near_dq", (nblk, WINDOW, HEAD), BF16)
    vmem("df_t", (width, nblk * WINDOW), BF16)
    vmem("heads_t", (width, nblk * WINDOW), BF16)
    if nblk <= ROOMY:
        vmem("a1_t", (layers, width, nblk * WINDOW), BF16)
        vmem("a2_t", (layers, width, nblk * WINDOW), BF16)
        vmem("w_qkv_t", (layers, 3 * width, width), BF16)
        vmem("w_out_t", (layers, width, width), BF16)
        vmem("w_up_t", (layers, hidden, width), BF16)
        vmem("w_down_t", (layers, width, hidden), BF16)
    vmem("near_order", (2, WINDOW, 2 * WINDOW), jnp.int32)
    vmem("far_order", (far_rows, far_rows), jnp.int32)
    vmem("sums", (layers, 4, 8, width), F32)
    vmem("grad", (layers, rows, CHUNK), F32)
    vmem("final", (layers, rows, CHUNK), BF16)
    vmem("got_core", (layers, rows // 2, CHUNK), BF16)
    vmem("got_batch", (layers, nb, rows // 2 // nb, CHUNK), BF16)
    vmem("got_pair", (layers, rows // 4 // nb, CHUNK), BF16)
    top = max(nw.bit_length() - 3, 1)
    vmem("got_top", (layers, top, rows // 4 // nb, CHUNK), BF16)
    vmem("put_core", (first_rows(nb, hidden) // 2, CHUNK), BF16)
    vmem("put_batch", (rows // 2, CHUNK), BF16)
    vmem("put_pair", (rows // 4 // nb, CHUNK), BF16)
    vmem("put_top", (top, rows // 4 // nb, CHUNK), BF16)
    vmem("norm_all", (nw, 4 * layers, width), F32)
    vmem("norm_batch", (nb, 4 * layers, width), F32)
    for name in ("in", "cot", "out", "gi"):
        sems(name + "_s", ns, nw)
        sems(name + "_r", ns, nw)
    sems("own", 4, ns)
    sems("load", 4)
    sems("save", layers, 2)
    for name, count in (("core", 1), ("batch", nb), ("pair", 1), ("top", top), ("pair_back", 1), ("batch_back", nb), ("core_back", 1)):
        sems(name + "_s", layers, 2, count)
        sems(name + "_r", layers, 2, count)
    sems("norm_all_s", nw)
    sems("norm_all_r", nw)
    sems("norm_batch_s", nb)
    sems("norm_batch_r", nb)
    return pieces


def kernel(nb, nw, ns, names, *refs):
    (lens, x_hbm, cot_hbm, gain1, bias1, gain2, bias2, wq_hbm, wo_hbm, wu_hbm, wd_hbm,
     out_hbm, gi_hbm, grads_hbm, norm_out) = refs[:15]
    m = types.SimpleNamespace(**dict(zip(names, refs[15:])))
    layers, width = gain1.shape
    hidden = wu_hbm.shape[2]
    per = x_hbm.shape[2]
    nblk = nw * per
    tiles = nblk // TILE
    groups = WINDOW // GROUP
    near_each = nblk // groups
    scale = float(HEAD) ** (-0.5)
    factor = scale * LOG2E
    me = lax.axis_index("wide")
    mb = lax.axis_index("batch")

    barrier = pltpu.get_barrier_semaphore()
    for k in range(1, nw):
        pl.semaphore_signal(barrier, inc=1, device_id=(mb, lax.rem(me + k, nw)), device_id_type=MESH)
    for k in range(1, nb):
        pl.semaphore_signal(barrier, inc=1, device_id=(lax.rem(mb + k, nb), me), device_id_type=MESH)
    pl.semaphore_wait(barrier, nw + nb - 2)

    def partner(k):
        place = me
        for bit in range(nw.bit_length() - 1):
            size = 2**bit
            if k & size:
                place = place + size - 2 * size * lax.rem(me // size, 2)
        return place

    far = [nw // 2 + k for k in range(nw // 2)]
    close = [k for k in range(nw // 2 - 1, 0, -1)]
    turns = [turn for pair in zip(far, close) for turn in pair] + [far[-1]]

    def gather_copy(src, dst, send, recv, s, other, owner):
        return pltpu.make_async_remote_copy(
            src_ref=src.at[other, s],
            dst_ref=dst.at[pl.ds(s * nblk + owner * per, per)],
            send_sem=send.at[s, other],
            recv_sem=recv.at[s, owner],
            device_id=(mb, other),
            device_id_type=MESH,
        )

    def gather_own(src, dst, which, s):
        return pltpu.make_async_copy(
            src.at[me, s], dst.at[pl.ds(s * nblk + me * per, per)], m.own.at[which, s]
        )

    def gather_start(src, dst, send, recv, which, s):
        for k in turns:
            gather_copy(src, dst, send, recv, s, partner(k), me).start()
        gather_own(src, dst, which, s).start()

    def gather_wait(src, dst, send, recv, which, s, steps=None):
        for k in range(1, nw) if steps is None else steps:
            other = partner(k)
            gather_copy(src, dst, send, recv, s, other, other).wait_recv()
        if steps is None or steps is close:
            gather_own(src, dst, which, s).wait()

    def gather_end(src, dst, send, recv, s):
        for k in range(1, nw):
            gather_copy(src, dst, send, recv, s, partner(k), me).wait_send()

    def scatter_copy(src, dst, send, recv, s, other, owner):
        return pltpu.make_async_remote_copy(
            src_ref=src.at[pl.ds(s * nblk + other * per, per)],
            dst_ref=dst.at[owner, s],
            send_sem=send.at[s, other],
            recv_sem=recv.at[s, owner],
            device_id=(mb, other),
            device_id_type=MESH,
        )

    def scatter_own(src, dst, which, s):
        return pltpu.make_async_copy(
            src.at[pl.ds(s * nblk + me * per, per)], dst.at[me, s], m.own.at[which, s]
        )

    def scatter_start(src, dst, send, recv, which, s, steps=None):
        for k in turns if steps is None else steps:
            scatter_copy(src, dst, send, recv, s, partner(k), me).start()
        if steps is None or steps is close:
            scatter_own(src, dst, which, s).start()

    def scatter_end(src, dst, send, recv, which, s):
        for k in range(1, nw):
            scatter_copy(src, dst, send, recv, s, partner(k), me).wait_send()
        for k in range(1, nw):
            other = partner(k)
            scatter_copy(src, dst, send, recv, s, other, other).wait_recv()
        scatter_own(src, dst, which, s).wait()

    ins = (x_hbm, m.x_in, m.in_s, m.in_r)
    cots = (cot_hbm, m.cot_in, m.cot_s, m.cot_r)
    outs = (m.x_in, out_hbm, m.out_s, m.out_r)
    gis = (m.cot_in, gi_hbm, m.gi_s, m.gi_r)

    gather_start(*ins, 0, 0)
    loads = [
        pltpu.make_async_copy(src, dst, m.load.at[i])
        for i, (src, dst) in enumerate(
            ((wq_hbm, m.w_qkv), (wo_hbm, m.w_out), (wu_hbm, m.w_up), (wd_hbm, m.w_down))
        )
    ]
    for load in loads:
        load.start()

    def orders(rows, columns, earlier, same, position):
        row = lax.broadcasted_iota(jnp.int32, (rows, columns), 0)
        column = lax.broadcasted_iota(jnp.int32, (rows, columns), 1)
        own = jnp.where(earlier(row, column), position(column), FAR)
        return jnp.where(same(row, column), -FAR, own)

    def near(lowest):
        return orders(
            WINDOW,
            2 * WINDOW,
            lambda r, c: (c < r + WINDOW) & (c > r) & (c >= lowest),
            lambda r, c: c == r + WINDOW,
            lambda c: c,
        )

    m.near_order[0] = near(WINDOW)
    m.near_order[1] = near(0)
    far_rows = nblk * GROUP
    m.far_order[...] = orders(
        far_rows,
        far_rows,
        lambda r, c: (c < r) & (((r - c) & (GROUP - 1)) == 0),
        lambda r, c: c == r,
        lambda c: (c // GROUP) * WINDOW + (c & (GROUP - 1)),
    )
    m.sums[...] = jnp.zeros_like(m.sums)
    for load in loads:
        load.wait()
    roomy = nblk <= ROOMY
    for l in range(layers if roomy else 0):
        m.w_out_t[l] = m.w_out[l].T
        for c in range(3):
            part = slice(c * CHUNK, (c + 1) * CHUNK)
            m.w_qkv_t[l, part] = m.w_qkv[l, :, part].T
        for c in range(hidden // CHUNK):
            part = slice(c * CHUNK, (c + 1) * CHUNK)
            m.w_up_t[l, part] = m.w_up[l, :, part].T
            m.w_down_t[l, :, part] = m.w_down[l, part].T

    def rows_of(t):
        return pl.ds(t * TILE, TILE)

    def back_dot(x, name, l):
        if roomy:
            return dot(x, getattr(m, name + "_t")[l])
        return dot_nt(x, getattr(m, name)[l])

    def lanes_of(t):
        return pl.ds(pl.multiple_of(t * TILE * WINDOW, TILE * WINDOW), TILE * WINDOW)

    def cols(c):
        return slice(c * CHUNK, (c + 1) * CHUNK)

    def loop(count, body, unroll=1):
        unroll = min(unroll, count)

        def step(i, carry):
            for e in range(unroll):
                body(i * unroll + e)
            return carry

        lax.fori_loop(0, count // unroll, step, 0)

    def near_tiles(i):
        return [i * AT_ONCE * near_each + e for e in range(AT_ONCE * near_each)]

    def far_tiles(i):
        return [i * AT_ONCE + e for e in range(AT_ONCE)]

    def window(ref, b, part):
        return jnp.concatenate([ref[jnp.maximum(b - 1, 0), :, part], ref[b, :, part]], axis=0)

    def spread(i):
        return pl.ds(pl.multiple_of(i * GROUP, GROUP), GROUP)

    def strided(v):
        return v.astype(BF16).reshape(nblk, GROUP, HEAD)

    def halves_of(t):
        step = TILE if roomy else 2
        return [pl.ds(t * TILE + i, step) for i in range(0, TILE, step)]

    def parts_of(rows):
        each = WINDOW // PIECE
        return [
            (rows.start + i // each, slice(i % each * PIECE, (i % each + 1) * PIECE), slice(i * PIECE, (i + 1) * PIECE))
            for i in range(rows.size * each)
        ]

    def store_norm(l, which, b, r, x, normed, gain, bias):
        hat, inverse = normalize(x)
        k = 2 * l + which
        m.stats[b, r, k : k + 1] = inverse
        normed[l, b, r] = (hat * gain[l : l + 1] + bias[l : l + 1]).astype(BF16)

    def source(l, s, b, r):
        if l == 0:
            return m.x_in[s * nblk + b, r].astype(F32)
        return m.dx[b, r]

    def forward(l, s):
        length = lens[me * ns + s]

        def project(t):
            for b, r, _ in parts_of(rows_of(t)):
                store_norm(l, 0, b, r, source(l, s, b, r), m.a1, gain1, bias1)
            rows = rows_of(t)
            a = flat(m.a1[l, rows])
            if roomy:
                m.a1_t[l, :, lanes_of(t)] = a.T
            m.qkv[l, rows] = blocks(dot(a, m.w_qkv[l]).astype(BF16))

        here = m.qkv.at[l]

        def attend(i):
            scores = [
                dot_nt(here[b, :, Q_NEAR], window(here, b, K_NEAR)) for b in near_tiles(i)
            ] + [dot_nt(flat(here[:, spread(j), Q_FAR]), flat(here[:, spread(j), K_FAR])) for j in far_tiles(i)]
            rules = [
                (m.near_order.at[jnp.minimum(b, 1)], length - (b - 1) * WINDOW) for b in near_tiles(i)
            ] + [(m.far_order, length - j * GROUP) for j in far_tiles(i)]
            p = [weights_of(x, *rule, factor) for x, rule in zip(scores, rules)]
            for b, x in zip(near_tiles(i), p):
                m.near_p[l, b] = x
                result = dot(x, window(here, b, V_NEAR))
                m.heads[l, b, :, 0:HEAD] = result.astype(BF16)
            for j, x in zip(far_tiles(i), p[len(near_tiles(i)) :]):
                m.far_p[l, j] = x
                result = dot(x, flat(here[:, spread(j), V_FAR]))
                m.heads[l, :, spread(j), HEAD:] = strided(result)

        def mix(t):
            rows = rows_of(t)
            mixed = dot(flat(m.heads[l, rows]), m.w_out[l])
            for b, r, i in parts_of(rows_of(t)):
                y = source(l, s, b, r) + mixed[i]
                m.dx[b, r] = y
                store_norm(l, 1, b, r, y, m.a2, gain2, bias2)
            if roomy:
                m.a2_t[l, :, lanes_of(t)] = flat(m.a2[l, rows]).T
            for half in halves_of(t):
                h = dot(flat(m.a2[l, half]), m.w_up[l])
                for b, r, i in parts_of(half):
                    for c in range(hidden // CHUNK):
                        m.act[l, b, r, cols(c)], m.slope[l, b, r, cols(c)] = gelu_pair(h[i, cols(c)])
            fed = dot(flat(m.act[l, rows]), m.w_down[l])
            for b, r, i in parts_of(rows_of(t)):
                y = m.dx[b, r] + fed[i]
                if l == layers - 1:
                    m.x_in[s * nblk + b, r] = y.astype(BF16)
                else:
                    m.dx[b, r] = y

        loop(tiles, project)
        loop(groups // AT_ONCE, attend)
        loop(tiles, mix)

    def unnorm(l, which, b, r, grad, normed, gain, bias, over):
        hat = (normed[l, b, r].astype(F32) - bias[l : l + 1]) * over
        k = 2 * l + which
        back = norm_back(grad, hat, m.stats[b, r, k : k + 1], gain[l : l + 1])
        return back, row_sums(grad * hat), row_sums(grad)

    def add_sums(l, which, terms):
        for k in range(2):
            total = terms[0][k]
            for term in terms[1:]:
                total = total + term[k]
            m.sums[l, 2 * which + k] += total

    def back_feed(l, s):
        def body(t):
            rows = rows_of(t)
            source = m.cot_in.at[pl.ds(s * nblk, nblk)] if l == layers - 1 else m.dx
            for b, r, _ in parts_of(rows_of(t)):
                m.df[b, r] = source[b, r].astype(BF16)
            m.df_t[:, lanes_of(t)] = flat(m.df[rows]).T
            m.heads_t[:, lanes_of(t)] = flat(m.heads[l, rows]).T
            for half in halves_of(t):
                dg = back_dot(flat(m.df[half]), "w_down", l)
                for b, r, i in parts_of(half):
                    for c in range(hidden // CHUNK):
                        slope = m.slope[l, b, r, cols(c)].astype(F32)
                        m.slope[l, b, r, cols(c)] = (dg[i, cols(c)] * slope).astype(BF16)
            da = back_dot(flat(m.slope[l, rows]), "w_up", l)
            over = 1.0 / gain2[l : l + 1]
            terms = []
            for b, r, i in parts_of(rows_of(t)):
                back, *term = unnorm(l, 1, b, r, da[i], m.a2, gain2, bias2, over)
                terms.append(term)
                dy = source[b, r].astype(F32) + back
                m.dx[b, r] = dy
                m.dm[b, r] = dy.astype(BF16)
            add_sums(l, 1, terms)
            do = back_dot(flat(m.dm[rows]), "w_out", l)
            m.do[pl.ds(t * TILE, TILE)] = blocks(do.astype(BF16))

        loop(tiles, body)

    def back_scores(p, dp):
        parts = []
        for r in pieces_of(dp.shape[0]):
            high = p[r].astype(F32)
            inner = jnp.sum(dp[r] * high, axis=1, keepdims=True)
            parts.append((high * (dp[r] - inner)).astype(BF16))
        return jnp.concatenate(parts, axis=0)

    def back_attend(l, s):
        here = m.qkv.at[l]
        near_p = m.near_p.at[l]

        def body(i):
            near, far = near_tiles(i), far_tiles(i)
            far_do = [flat(m.do[:, spread(j), HEAD:]) for j in far]
            far_p = [m.far_p[l, j] for j in far]
            dp = [dot_nt(m.do[b, :, 0:HEAD], window(here, b, V_NEAR)) for b in near]
            dp += [dot_nt(x, flat(here[:, spread(j), V_FAR])) for j, x in zip(far, far_do)]
            p = [near_p[b] for b in near] + far_p
            ds = [back_scores(x, y) for x, y in zip(p, dp)]
            for b, x in zip(near, ds):
                m.near_ds[b] = x
                m.near_dq[b] = (dot(x, window(here, b, K_NEAR)) * scale).astype(BF16)
            for j, do, w, x in zip(far, far_do, far_p, ds[len(near) :]):
                q = flat(here[:, spread(j), Q_FAR])
                dq = dot(x, flat(here[:, spread(j), K_FAR])) * scale
                dk = dot_tn(x, q) * scale
                dv = dot_tn(w, do)
                here[:, spread(j), Q_FAR] = strided(dq)
                here[:, spread(j), K_FAR] = strided(dk)
                here[:, spread(j), V_FAR] = strided(dv)

        loop(groups // AT_ONCE, body)
        for b in range(nblk):
            if b + 1 < nblk:
                both = slice(b, b + 2)
                ds = jnp.concatenate([m.near_ds[b, :, WINDOW:], m.near_ds[b + 1, :, :WINDOW]], axis=0)
                p = jnp.concatenate([near_p[b, :, WINDOW:], near_p[b + 1, :, :WINDOW]], axis=0)
                q, do = flat(here[both, :, Q_NEAR]), flat(m.do[both, :, 0:HEAD])
            else:
                ds, p = m.near_ds[b, :, WINDOW:], near_p[b, :, WINDOW:]
                q, do = here[b, :, Q_NEAR], m.do[b, :, 0:HEAD]
            here[b, :, K_NEAR] = (dot_tn(ds, q) * scale).astype(BF16)
            here[b, :, V_NEAR] = dot_tn(p, do).astype(BF16)
            here[b, :, Q_NEAR] = m.near_dq[b]

    def back_project(l, s):
        def body(t):
            da = back_dot(flat(m.qkv[l, rows_of(t)]), "w_qkv", l)
            over = 1.0 / gain1[l : l + 1]
            terms = []
            for b, r, i in parts_of(rows_of(t)):
                back, *term = unnorm(l, 0, b, r, da[i], m.a1, gain1, bias1, over)
                terms.append(term)
                if l == 0:
                    m.cot_in[s * nblk + b, r] = (m.dx[b, r] + back).astype(BF16)
                else:
                    m.dx[b, r] = m.dx[b, r] + back
            add_sums(l, 0, terms)

        loop(tiles, body)

    def outer(l, s, left, ref, first, flipped=False):
        if len(left.shape) == 2:
            product = dot(left[...], flat(ref[...]))
        else:
            product = dot_tn(flat(left[...]), flat(ref[...]))
        for c in range(product.shape[1] // CHUNK):
            part = product[:, cols(c)]
            part = part.T if flipped else part
            if s > 0:
                part = part + m.grad[l, cols(first + c)]
            m.grad[l, cols(first + c)] = part

    def grads_feed(l, s):
        outer(l, s, (m.a2_t if roomy else m.a2).at[l], m.slope.at[l], 0)
        outer(l, s, m.df_t, m.act.at[l], hidden // CHUNK, True)
        outer(l, s, m.heads_t, m.dm, 2 * hidden // CHUNK)

    def grads_attend(l, s):
        outer(l, s, (m.a1_t if roomy else m.a1).at[l], m.qkv.at[l], 2 * hidden // CHUNK + 1)

    core = lax.rem(me, 2)
    second = lax.rem(me // 2, 2)
    bits = nw.bit_length() - 1

    def toggled(bit):
        size = 2**bit
        return me + size - 2 * size * lax.rem(me // size, 2)

    split = first_rows(nb, hidden)

    def reduction(l, which):
        start, count = ((0, split), (split, 12 * CHUNK - split))[which]
        half, chunk, piece = count // 2, count // 2 // nb, count // 4 // nb
        lead = start // 2
        final = m.final.at[l]

        def span(at, size):
            return pl.ds(pl.multiple_of(at, 16), size)

        mine = start + core * half
        theirs = start + (1 - core) * half
        chunk_at = mine + mb * chunk
        piece_at = chunk_at + second * piece
        other_piece = chunk_at + (1 - second) * piece
        core_in = m.got_core.at[l, pl.ds(lead, half)]

        def remote(src, dst, name, k_send, k_recv, device):
            return pltpu.make_async_remote_copy(
                src_ref=src,
                dst_ref=dst,
                send_sem=getattr(m, name + "_s").at[l, which, k_send],
                recv_sem=getattr(m, name + "_r").at[l, which, k_recv],
                device_id=device,
                device_id_type=MESH,
            )

        def here(at, size):
            return final.at[span(at, size)]

        to_core = remote(m.put_core.at[pl.ds(0, half)], core_in, "core", 0, 0, (mb, toggled(0)))
        to_pair = remote(
            m.put_pair.at[pl.ds(start // 4 // nb, piece)],
            m.got_pair.at[l, pl.ds(start // 4 // nb, piece)],
            "pair", 0, 0, (mb, toggled(1)),
        )

        def to_batch(other, owner):
            return remote(
                m.put_batch.at[span(lead + other * chunk, chunk)],
                m.got_batch.at[l, owner, pl.ds(start // 2 // nb, chunk)],
                "batch", other, owner, (other, me),
            )

        def to_top(bit):
            return remote(
                m.put_top.at[bit - 2, pl.ds(start // 4 // nb, piece)],
                m.got_top.at[l, bit - 2, pl.ds(start // 4 // nb, piece)],
                "top", bit - 2, bit - 2, (mb, toggled(bit)),
            )

        def pair_back(at):
            return remote(here(at, piece), here(at, piece), "pair_back", 0, 0, (mb, toggled(1)))

        def batch_back(other, owner):
            at = mine + owner * chunk
            return remote(here(at, chunk), here(at, chunk), "batch_back", other, owner, (other, me))

        def core_back(at):
            return remote(here(at, half), here(at, half), "core_back", 0, 0, (mb, toggled(0)))

        def others():
            return [lax.rem(mb + k, nb) for k in range(1, nb)]

        def step0():
            m.put_core[pl.ds(0, half)] = m.grad[l, span(theirs, half)].astype(BF16)
            to_core.start()

        def step1():
            to_core.wait()
            total = m.grad[l, span(mine, half)] + m.got_core[l, pl.ds(lead, half)].astype(F32)
            m.grad[l, span(mine, half)] = total
            m.put_batch[pl.ds(lead, half)] = total.astype(BF16)
            for other in others():
                to_batch(other, mb).start()

        def step2():
            total = m.grad[l, span(chunk_at, chunk)]
            for other in others():
                to_batch(other, mb).wait_send()
                to_batch(other, other).wait_recv()
                got = m.got_batch[l, other, pl.ds(start // 2 // nb, chunk)]
                total = total + got.astype(F32)
            m.grad[l, span(chunk_at, chunk)] = total
            send = m.grad[l, span(other_piece, piece)]
            m.put_pair[pl.ds(start // 4 // nb, piece)] = send.astype(BF16)
            to_pair.start()

        def step3():
            to_pair.wait()
            got = m.got_pair[l, pl.ds(start // 4 // nb, piece)]
            total = m.grad[l, span(piece_at, piece)] + got.astype(F32)
            m.put_top[0, pl.ds(start // 4 // nb, piece)] = total.astype(BF16)
            to_top(2).start()

        def step4(bit=2):
            to_top(bit).wait()
            at = pl.ds(start // 4 // nb, piece)
            total = m.put_top[bit - 2, at].astype(F32) + m.got_top[l, bit - 2, at].astype(F32)
            if bit + 1 < bits:
                m.put_top[bit - 1, at] = total.astype(BF16)
                to_top(bit + 1).start()
                step4(bit + 1)
            else:
                final[span(piece_at, piece)] = total.astype(BF16)
                pair_back(piece_at).start()

        def step5():
            pair_back(other_piece).wait_recv()
            for other in others():
                batch_back(other, mb).start()

        def step6():
            for other in others():
                batch_back(other, other).wait_recv()
            core_back(mine).start()

        save = pltpu.make_async_copy(
            final.at[pl.ds(start, count)],
            grads_hbm.at[l, pl.ds(start, count)],
            m.save.at[l, which],
        )

        def step7():
            core_back(theirs).wait_recv()
            save.start()

        def step8():
            pair_back(piece_at).wait_send()
            for other in others():
                batch_back(other, mb).wait_send()
            core_back(mine).wait_send()
            save.wait()

        return [step0, step1, step2, step3, step4, step5, step6, step7, step8]

    sums = {(l, w): reduction(l, w) for l in range(layers) for w in range(2)}
    waiting = []

    def advance():
        for steps in waiting[::-1]:
            steps.pop(0)()
            if not steps:
                waiting.remove(steps)

    def begin(l, which, last):
        if last:
            steps = sums[l, which]
            steps.pop(0)()
            waiting.append(steps)

    for s in range(ns):
        last = s == ns - 1
        gather_wait(*ins, 0, s, close)
        gather_wait(*ins, 0, s, far[: len(far) // 2])
        if s == 0:
            gather_start(*cots, 1, s)
        gather_wait(*ins, 0, s, far[len(far) // 2 :])
        for l in range(layers):
            with jax.named_scope("layer_forward"):
                forward(l, s)
        gather_wait(*cots, 1, s)
        if not last:
            gather_start(*ins, 0, s + 1)
        else:
            scatter_start(*outs, 2, s)
        for l in reversed(range(layers)):
            with jax.named_scope("feed_backward"):
                back_feed(l, s)
            if l < layers - 1:
                advance()
            with jax.named_scope("feed_gradients"):
                grads_feed(l, s)
            begin(l, 0, last)
            with jax.named_scope("attention_backward"):
                back_attend(l, s)
            advance()
            if not last:
                if l == layers - 1:
                    gather_start(*cots, 1, s + 1)
                if l == 0:
                    scatter_start(*outs, 2, s)
            with jax.named_scope("attention_gradients"):
                grads_attend(l, s)
            begin(l, 1, last)
            with jax.named_scope("input_backward"):
                back_project(l, s)
            if l == 0:
                advance()
        if not last:
            scatter_start(*gis, 3, s)
    scatter_start(*gis, 3, ns - 1, far[: len(far) // 2])
    scatter_start(*gis, 3, ns - 1, close)

    def norm_copy(own, slots, k, device, name, owner):
        return pltpu.make_async_remote_copy(
            src_ref=slots.at[own],
            dst_ref=slots.at[owner],
            send_sem=getattr(m, name + "_s").at[k],
            recv_sem=getattr(m, name + "_r").at[owner],
            device_id=device,
            device_id_type=MESH,
        )

    m.norm_all[me] = jnp.sum(m.sums[...].reshape(4 * layers, 8, width), axis=1)
    for k in range(1, nw):
        other = lax.rem(me + k, nw)
        norm_copy(me, m.norm_all, other, (mb, other), "norm_all", me).start()
    for _ in range(3):
        advance()
    scatter_start(*gis, 3, ns - 1, far[len(far) // 2 :])
    for k in range(1, nw):
        other = lax.rem(me + k, nw)
        norm_copy(me, m.norm_all, other, (mb, other), "norm_all", other).wait_recv()
    total = m.norm_all[0]
    for k in range(1, nw):
        total = total + m.norm_all[k]
    m.norm_batch[mb] = total
    for k in range(1, nb):
        other = lax.rem(mb + k, nb)
        norm_copy(mb, m.norm_batch, other, (other, me), "norm_batch", mb).start()
    while waiting:
        advance()
    for k in range(1, nb):
        other = lax.rem(mb + k, nb)
        norm_copy(mb, m.norm_batch, other, (other, me), "norm_batch", other).wait_recv()
    total = m.norm_batch[0]
    for k in range(1, nb):
        total = total + m.norm_batch[k]
    norm_out[...] = total

    for k in range(1, nw):
        other = lax.rem(me + k, nw)
        norm_copy(me, m.norm_all, other, (mb, other), "norm_all", me).wait_send()
    for k in range(1, nb):
        other = lax.rem(mb + k, nb)
        norm_copy(mb, m.norm_batch, other, (other, me), "norm_batch", mb).wait_send()
    for s in range(ns):
        gather_end(*ins, s)
        gather_end(*cots, s)
        scatter_end(*outs, 2, s)
        scatter_end(*gis, 3, s)


def per_device(nb, nw, inputs, lengths, gain1, bias1, w_qkv, w_out, gain2, bias2, w_up, w_down, cotangent):
    count, block, width = inputs.shape
    layers, _, hidden = w_up.shape
    ns, per = count // nw, block // WINDOW
    pieces = plan(nb, nw, ns, nw * per, width, hidden, layers)
    shape = (nw, ns, per, WINDOW, width)
    anywhere = pl.BlockSpec(memory_space=pl.ANY)
    vmem = pl.BlockSpec(memory_space=pltpu.VMEM)
    rows = 12 * CHUNK

    def body(*refs):
        kernel(nb, nw, ns, list(pieces), *refs)

    outputs, grad_rows, grads, norms = pl.pallas_call(
        body,
        out_shape=(
            jax.ShapeDtypeStruct(shape, BF16),
            jax.ShapeDtypeStruct(shape, BF16),
            jax.ShapeDtypeStruct((layers, rows, CHUNK), BF16),
            jax.ShapeDtypeStruct((4 * layers, width), F32),
        ),
        in_specs=[pl.BlockSpec(memory_space=pltpu.SMEM)] + [anywhere] * 2 + [vmem] * 4 + [anywhere] * 4,
        out_specs=(anywhere, anywhere, anywhere, vmem),
        scratch_shapes=list(pieces.values()),
        compiler_params=pltpu.CompilerParams(
            collective_id=0, has_side_effects=True, vmem_limit_bytes=64 * 1024 * 1024
        ),
    )(
        lengths, inputs.reshape(shape), cotangent.reshape(shape),
        gain1, bias1, gain2, bias2, w_qkv, w_out, w_up, w_down,
    )
    each = hidden // CHUNK
    tokens = count * block // layers

    def finish(out_in, rows_in, grads_in, norm_in, *results):
        out_out, rows_out, qkv_out, rest_out, up_out, down_out, *norm_outs = results
        out_out[...] = out_in[...]
        rows_out[...] = rows_in[...].astype(F32)

        def part(c):
            return grads_in[0, c * CHUNK : (c + 1) * CHUNK].astype(F32)

        for c in range(each):
            up_out[0, :, c * CHUNK : (c + 1) * CHUNK] = part(c)
            down_out[0, c * CHUNK : (c + 1) * CHUNK] = part(each + c)
        rest_out[0] = part(2 * each)
        for c in range(3):
            qkv_out[0, :, c * CHUNK : (c + 1) * CHUNK] = part(2 * each + 1 + c)
        for l in range(layers):
            for k in range(4):
                norm_outs[k][l : l + 1] = norm_in[4 * l + k : 4 * l + k + 1]

    row_spec = pl.BlockSpec((tokens, width), lambda i: (i, 0))
    norm_spec = pl.BlockSpec((layers, width), lambda i: (0, 0))

    def layer_spec(*dims):
        return pl.BlockSpec((1, *dims), lambda i: (i, 0, 0))

    outputs, grad_rows, grad_qkv, grad_out, grad_up, grad_down, *norms = pl.pallas_call(
        finish,
        grid=(layers,),
        out_shape=(
            jax.ShapeDtypeStruct((count * block, width), BF16),
            jax.ShapeDtypeStruct((count * block, width), F32),
            jax.ShapeDtypeStruct((layers, width, 3 * width), F32),
            jax.ShapeDtypeStruct((layers, width, width), F32),
            jax.ShapeDtypeStruct((layers, width, hidden), F32),
            jax.ShapeDtypeStruct((layers, hidden, width), F32),
        )
        + (jax.ShapeDtypeStruct((layers, width), F32),) * 4,
        in_specs=[
            row_spec,
            row_spec,
            layer_spec(rows, CHUNK),
            pl.BlockSpec((4 * layers, width), lambda i: (0, 0)),
        ],
        out_specs=(
            row_spec,
            row_spec,
            layer_spec(width, 3 * width),
            layer_spec(width, width),
            layer_spec(width, hidden),
            layer_spec(hidden, width),
        )
        + (norm_spec,) * 4,
        compiler_params=pltpu.CompilerParams(vmem_limit_bytes=60 * 1024 * 1024),
    )(outputs.reshape(count * block, width), grad_rows.reshape(count * block, width), grads, norms)
    return (
        outputs.reshape(count, block, width),
        grad_rows.reshape(count, block, width),
        norms[0],
        norms[1],
        grad_qkv,
        grad_out,
        norms[2],
        norms[3],
        grad_up,
        grad_down,
    )


def solution(mesh):
    nb, nw = mesh.shape["batch"], mesh.shape["wide"]

    def step(*args):
        return per_device(nb, nw, *args)

    rows = P("batch", "wide", None)
    return jax.shard_map(
        step,
        mesh=mesh,
        in_specs=(rows, P("batch")) + (P(),) * 8 + (rows,),
        out_specs=(rows, rows) + (P(),) * 8,
        check_vma=False,
    )
```

```python
import types

import jax
import jax.numpy as jnp
from jax import lax
from jax.experimental import pallas as pl
from jax.experimental.pallas import tpu as pltpu
from jax.sharding import PartitionSpec as P

MESH = pl.DeviceIdType.MESH
F32, BF16 = jnp.float32, jnp.bfloat16
HEAD = 128
WINDOW = 128
GROUP = 16
TILE = 4
PIECE = 32
CHUNK = 256
ROOMY = 8
AT_ONCE = 4
Q_NEAR, Q_FAR, K_NEAR, K_FAR, V_NEAR, V_FAR = (slice(i * HEAD, (i + 1) * HEAD) for i in range(6))
FAR = 1 << 20
MASKED = -1e30
LOG2E = 1.4426950408889634
GELU_A = 0.7978845608028654
GELU_B = GELU_A * 0.044715


def dot(a, b):
    return lax.dot_general(a, b, (((1,), (0,)), ((), ())), preferred_element_type=F32)


def dot_nt(a, b):
    return lax.dot_general(a, b, (((1,), (1,)), ((), ())), preferred_element_type=F32)


def dot_tn(a, b):
    return lax.dot_general(a, b, (((0,), (0,)), ((), ())), preferred_element_type=F32)


def flat(v):
    return v.reshape(-1, v.shape[-1])


def blocks(v):
    return v.reshape(-1, WINDOW, v.shape[-1])


def normalize(x):
    center = x - jnp.mean(x, axis=-1, keepdims=True)
    inverse = lax.rsqrt(jnp.mean(center * center, axis=-1, keepdims=True) + 1e-05)
    return center * inverse, inverse


def norm_back(grad, hat, inverse, gain):
    scaled = grad * gain
    first = jnp.mean(scaled, axis=-1, keepdims=True)
    second = jnp.mean(scaled * hat, axis=-1, keepdims=True)
    return inverse * (scaled - first - hat * second)


def row_sums(v):
    return jnp.sum(v.reshape(-1, 8, v.shape[-1]), axis=0)


def pieces_of(rows):
    return [slice(i, i + PIECE) for i in range(0, rows, PIECE)]


def weights_of(scores, order, limit, factor):
    parts = []
    for r in pieces_of(scores.shape[0]):
        masked = jnp.where(order[r] < limit, scores[r], MASKED)
        peak = jnp.max(masked, axis=1, keepdims=True)
        powered = jnp.exp2((masked - peak) * factor)
        parts.append((powered * (1.0 / jnp.sum(powered, axis=1, keepdims=True))).astype(BF16))
    return jnp.concatenate(parts, axis=0)


def gelu_pair(h):
    square = h * h
    q = 0.5 * jnp.tanh(h * (GELU_B * square + GELU_A)) + 0.5
    g = h * q
    slope = q + g * (1.0 - q) * (6.0 * GELU_B * square + 2.0 * GELU_A)
    return g.astype(BF16), slope.astype(BF16)


def plan(nb, nw, ns, nblk, width, hidden, layers):
    total = ns * nblk
    far_rows = nblk * GROUP
    rows = 12 * CHUNK
    pieces = {}

    def vmem(name, dims, kind):
        pieces[name] = pltpu.VMEM(dims, kind)

    def sems(name, *dims):
        pieces[name] = pltpu.SemaphoreType.DMA(dims)

    vmem("x_in", (total, WINDOW, width), BF16)
    vmem("cot_in", (total, WINDOW, width), BF16)
    vmem("w_qkv", (layers, width, 3 * width), BF16)
    vmem("w_out", (layers, width, width), BF16)
    vmem("w_up", (layers, width, hidden), BF16)
    vmem("w_down", (layers, hidden, width), BF16)
    vmem("a1", (layers, nblk, WINDOW, width), BF16)
    vmem("a2", (layers, nblk, WINDOW, width), BF16)
    vmem("qkv", (layers, nblk, WINDOW, 3 * width), BF16)
    vmem("heads", (layers, nblk, WINDOW, width), BF16)
    vmem("near_p", (layers, nblk, WINDOW, 2 * WINDOW), BF16)
    vmem("far_p", (layers, WINDOW // GROUP, far_rows, far_rows), BF16)
    vmem("act", (layers, nblk, WINDOW, hidden), BF16)
    vmem("slope", (layers, nblk, WINDOW, hidden), BF16)
    vmem("stats", (nblk, WINDOW, WINDOW), F32)
    vmem("dx", (nblk, WINDOW, width), F32)
    vmem("df", (nblk, WINDOW, width), BF16)
    vmem("dm", (nblk, WINDOW, width), BF16)
    vmem("do", (nblk, WINDOW, width), BF16)
    vmem("near_ds", (nblk, WINDOW, 2 * WINDOW), BF16)
    vmem("near_dq", (nblk, WINDOW, HEAD), BF16)
    vmem("df_t", (width, nblk * WINDOW), BF16)
    vmem("heads_t", (width, nblk * WINDOW), BF16)
    if nblk <= ROOMY:
        vmem("a1_t", (layers, width, nblk * WINDOW), BF16)
        vmem("a2_t", (layers, width, nblk * WINDOW), BF16)
        vmem("w_qkv_t", (layers, 3 * width, width), BF16)
        vmem("w_out_t", (layers, width, width), BF16)
        vmem("w_up_t", (layers, hidden, width), BF16)
        vmem("w_down_t", (layers, width, hidden), BF16)
    vmem("near_order", (2, WINDOW, 2 * WINDOW), jnp.int32)
    vmem("far_order", (far_rows, far_rows), jnp.int32)
    vmem("sums", (layers, 4, 8, width), F32)
    vmem("grad", (layers, rows, CHUNK), F32)
    vmem("final", (layers, rows, CHUNK), BF16)
    vmem("got_core", (layers, rows // 2, CHUNK), BF16)
    vmem("got_batch", (layers, nb, rows // 2 // nb, CHUNK), BF16)
    vmem("got_pair", (layers, rows // 4 // nb, CHUNK), BF16)
    top = max(nw.bit_length() - 3, 1)
    vmem("got_top", (layers, top, rows // 4 // nb, CHUNK), BF16)
    vmem("put_core", (hidden + CHUNK // 2, CHUNK), BF16)
    vmem("put_batch", (hidden + CHUNK // 2, CHUNK), BF16)
    vmem("put_pair", (rows // 4 // nb, CHUNK), BF16)
    vmem("put_top", (top, rows // 4 // nb, CHUNK), BF16)
    vmem("norm_all", (nw, 4 * layers, width), F32)
    vmem("norm_batch", (nb, 4 * layers, width), F32)
    for name in ("in", "cot", "out", "gi"):
        sems(name + "_s", ns, nw)
        sems(name + "_r", ns, nw)
    sems("own", 4, ns)
    sems("load", 4)
    sems("save", layers, 2)
    for name, count in (("core", 1), ("batch", nb), ("pair", 1), ("top", top), ("pair_back", 1), ("batch_back", nb), ("core_back", 1)):
        sems(name + "_s", layers, 2, count)
        sems(name + "_r", layers, 2, count)
    sems("norm_all_s", nw)
    sems("norm_all_r", nw)
    sems("norm_batch_s", nb)
    sems("norm_batch_r", nb)
    return pieces


def kernel(nb, nw, ns, names, *refs):
    (lens, x_hbm, cot_hbm, gain1, bias1, gain2, bias2, wq_hbm, wo_hbm, wu_hbm, wd_hbm,
     out_hbm, gi_hbm, grads_hbm, norm_out) = refs[:15]
    m = types.SimpleNamespace(**dict(zip(names, refs[15:])))
    layers, width = gain1.shape
    hidden = wu_hbm.shape[2]
    per = x_hbm.shape[2]
    nblk = nw * per
    tiles = nblk // TILE
    groups = WINDOW // GROUP
    near_each = nblk // groups
    scale = float(HEAD) ** (-0.5)
    factor = scale * LOG2E
    me = lax.axis_index("wide")
    mb = lax.axis_index("batch")

    barrier = pltpu.get_barrier_semaphore()
    for k in range(1, nw):
        pl.semaphore_signal(barrier, inc=1, device_id=(mb, lax.rem(me + k, nw)), device_id_type=MESH)
    for k in range(1, nb):
        pl.semaphore_signal(barrier, inc=1, device_id=(lax.rem(mb + k, nb), me), device_id_type=MESH)
    pl.semaphore_wait(barrier, nw + nb - 2)

    def partner(k):
        place = me
        for bit in range(nw.bit_length() - 1):
            size = 2**bit
            if k & size:
                place = place + size - 2 * size * lax.rem(me // size, 2)
        return place

    far = [nw // 2 + k for k in range(nw // 2)]
    close = [k for k in range(nw // 2 - 1, 0, -1)]
    turns = [turn for pair in zip(far, close) for turn in pair] + [far[-1]]

    def gather_copy(src, dst, send, recv, s, other, owner):
        return pltpu.make_async_remote_copy(
            src_ref=src.at[other, s],
            dst_ref=dst.at[pl.ds(s * nblk + owner * per, per)],
            send_sem=send.at[s, other],
            recv_sem=recv.at[s, owner],
            device_id=(mb, other),
            device_id_type=MESH,
        )

    def gather_own(src, dst, which, s):
        return pltpu.make_async_copy(
            src.at[me, s], dst.at[pl.ds(s * nblk + me * per, per)], m.own.at[which, s]
        )

    def gather_start(src, dst, send, recv, which, s):
        for k in turns:
            gather_copy(src, dst, send, recv, s, partner(k), me).start()
        gather_own(src, dst, which, s).start()

    def gather_wait(src, dst, send, recv, which, s, steps=None):
        for k in range(1, nw) if steps is None else steps:
            other = partner(k)
            gather_copy(src, dst, send, recv, s, other, other).wait_recv()
        if steps is None or steps is close:
            gather_own(src, dst, which, s).wait()

    def gather_end(src, dst, send, recv, s):
        for k in range(1, nw):
            gather_copy(src, dst, send, recv, s, partner(k), me).wait_send()

    def scatter_copy(src, dst, send, recv, s, other, owner):
        return pltpu.make_async_remote_copy(
            src_ref=src.at[pl.ds(s * nblk + other * per, per)],
            dst_ref=dst.at[owner, s],
            send_sem=send.at[s, other],
            recv_sem=recv.at[s, owner],
            device_id=(mb, other),
            device_id_type=MESH,
        )

    def scatter_own(src, dst, which, s):
        return pltpu.make_async_copy(
            src.at[pl.ds(s * nblk + me * per, per)], dst.at[me, s], m.own.at[which, s]
        )

    def scatter_start(src, dst, send, recv, which, s, steps=None):
        for k in turns if steps is None else steps:
            scatter_copy(src, dst, send, recv, s, partner(k), me).start()
        if steps is None or steps is close:
            scatter_own(src, dst, which, s).start()

    def scatter_end(src, dst, send, recv, which, s):
        for k in range(1, nw):
            scatter_copy(src, dst, send, recv, s, partner(k), me).wait_send()
        for k in range(1, nw):
            other = partner(k)
            scatter_copy(src, dst, send, recv, s, other, other).wait_recv()
        scatter_own(src, dst, which, s).wait()

    ins = (x_hbm, m.x_in, m.in_s, m.in_r)
    cots = (cot_hbm, m.cot_in, m.cot_s, m.cot_r)
    outs = (m.x_in, out_hbm, m.out_s, m.out_r)
    gis = (m.cot_in, gi_hbm, m.gi_s, m.gi_r)

    gather_start(*ins, 0, 0)
    loads = [
        pltpu.make_async_copy(src, dst, m.load.at[i])
        for i, (src, dst) in enumerate(
            ((wq_hbm, m.w_qkv), (wo_hbm, m.w_out), (wu_hbm, m.w_up), (wd_hbm, m.w_down))
        )
    ]
    for load in loads:
        load.start()

    def orders(rows, columns, earlier, same, position):
        row = lax.broadcasted_iota(jnp.int32, (rows, columns), 0)
        column = lax.broadcasted_iota(jnp.int32, (rows, columns), 1)
        own = jnp.where(earlier(row, column), position(column), FAR)
        return jnp.where(same(row, column), -FAR, own)

    def near(lowest):
        return orders(
            WINDOW,
            2 * WINDOW,
            lambda r, c: (c < r + WINDOW) & (c > r) & (c >= lowest),
            lambda r, c: c == r + WINDOW,
            lambda c: c,
        )

    m.near_order[0] = near(WINDOW)
    m.near_order[1] = near(0)
    far_rows = nblk * GROUP
    m.far_order[...] = orders(
        far_rows,
        far_rows,
        lambda r, c: (c < r) & (((r - c) & (GROUP - 1)) == 0),
        lambda r, c: c == r,
        lambda c: (c // GROUP) * WINDOW + (c & (GROUP - 1)),
    )
    m.sums[...] = jnp.zeros_like(m.sums)
    for load in loads:
        load.wait()
    roomy = nblk <= ROOMY
    for l in range(layers if roomy else 0):
        m.w_out_t[l] = m.w_out[l].T
        for c in range(3):
            part = slice(c * CHUNK, (c + 1) * CHUNK)
            m.w_qkv_t[l, part] = m.w_qkv[l, :, part].T
        for c in range(hidden // CHUNK):
            part = slice(c * CHUNK, (c + 1) * CHUNK)
            m.w_up_t[l, part] = m.w_up[l, :, part].T
            m.w_down_t[l, :, part] = m.w_down[l, part].T

    def rows_of(t):
        return pl.ds(t * TILE, TILE)

    def back_dot(x, name, l):
        if roomy:
            return dot(x, getattr(m, name + "_t")[l])
        return dot_nt(x, getattr(m, name)[l])

    def lanes_of(t):
        return pl.ds(pl.multiple_of(t * TILE * WINDOW, TILE * WINDOW), TILE * WINDOW)

    def cols(c):
        return slice(c * CHUNK, (c + 1) * CHUNK)

    def loop(count, body, unroll=1):
        unroll = min(unroll, count)

        def step(i, carry):
            for e in range(unroll):
                body(i * unroll + e)
            return carry

        lax.fori_loop(0, count // unroll, step, 0)

    def near_tiles(i):
        return [i * AT_ONCE * near_each + e for e in range(AT_ONCE * near_each)]

    def far_tiles(i):
        return [i * AT_ONCE + e for e in range(AT_ONCE)]

    def window(ref, b, part):
        return jnp.concatenate([ref[jnp.maximum(b - 1, 0), :, part], ref[b, :, part]], axis=0)

    def spread(i):
        return pl.ds(pl.multiple_of(i * GROUP, GROUP), GROUP)

    def strided(v):
        return v.astype(BF16).reshape(nblk, GROUP, HEAD)

    def halves_of(t):
        step = TILE if roomy else 2
        return [pl.ds(t * TILE + i, step) for i in range(0, TILE, step)]

    def parts_of(rows):
        each = WINDOW // PIECE
        return [
            (rows.start + i // each, slice(i % each * PIECE, (i % each + 1) * PIECE), slice(i * PIECE, (i + 1) * PIECE))
            for i in range(rows.size * each)
        ]

    def store_norm(l, which, b, r, x, normed, gain, bias):
        hat, inverse = normalize(x)
        k = 2 * l + which
        m.stats[b, r, k : k + 1] = inverse
        normed[l, b, r] = (hat * gain[l : l + 1] + bias[l : l + 1]).astype(BF16)

    def source(l, s, b, r):
        if l == 0:
            return m.x_in[s * nblk + b, r].astype(F32)
        return m.dx[b, r]

    def forward(l, s):
        length = lens[me * ns + s]

        def project(rows, lanes):
            for b, r, _ in parts_of(rows):
                store_norm(l, 0, b, r, source(l, s, b, r), m.a1, gain1, bias1)
            a = flat(m.a1[l, rows])
            if roomy:
                m.a1_t[l, :, lanes] = a.T
            m.qkv[l, rows] = blocks(dot(a, m.w_qkv[l]).astype(BF16))

        here = m.qkv.at[l]

        def attend(i):
            scores = [
                dot_nt(here[b, :, Q_NEAR], window(here, b, K_NEAR)) for b in near_tiles(i)
            ] + [dot_nt(flat(here[:, spread(j), Q_FAR]), flat(here[:, spread(j), K_FAR])) for j in far_tiles(i)]
            rules = [
                (m.near_order.at[jnp.minimum(b, 1)], length - (b - 1) * WINDOW) for b in near_tiles(i)
            ] + [(m.far_order, length - j * GROUP) for j in far_tiles(i)]
            p = [weights_of(x, *rule, factor) for x, rule in zip(scores, rules)]
            for b, x in zip(near_tiles(i), p):
                m.near_p[l, b] = x
                result = dot(x, window(here, b, V_NEAR))
                m.heads[l, b, :, 0:HEAD] = result.astype(BF16)
            for j, x in zip(far_tiles(i), p[len(near_tiles(i)) :]):
                m.far_p[l, j] = x
                result = dot(x, flat(here[:, spread(j), V_FAR]))
                m.heads[l, :, spread(j), HEAD:] = strided(result)

        def mix(t):
            rows = rows_of(t)
            mixed = dot(flat(m.heads[l, rows]), m.w_out[l])
            for b, r, i in parts_of(rows_of(t)):
                y = source(l, s, b, r) + mixed[i]
                m.dx[b, r] = y
                store_norm(l, 1, b, r, y, m.a2, gain2, bias2)
            if roomy:
                m.a2_t[l, :, lanes_of(t)] = flat(m.a2[l, rows]).T
            for half in halves_of(t):
                h = dot(flat(m.a2[l, half]), m.w_up[l])
                for b, r, i in parts_of(half):
                    for c in range(hidden // CHUNK):
                        m.act[l, b, r, cols(c)], m.slope[l, b, r, cols(c)] = gelu_pair(h[i, cols(c)])
            fed = dot(flat(m.act[l, rows]), m.w_down[l])
            for b, r, i in parts_of(rows_of(t)):
                y = m.dx[b, r] + fed[i]
                if l == layers - 1:
                    m.x_in[s * nblk + b, r] = y.astype(BF16)
                else:
                    m.dx[b, r] = y

        if roomy:
            project(pl.ds(0, nblk), pl.ds(0, nblk * WINDOW))
        else:
            loop(tiles, lambda t: project(rows_of(t), lanes_of(t)))
        loop(groups // AT_ONCE, attend)
        loop(tiles, mix)

    def unnorm(l, which, b, r, grad, normed, gain, bias, over):
        hat = (normed[l, b, r].astype(F32) - bias[l : l + 1]) * over
        k = 2 * l + which
        back = norm_back(grad, hat, m.stats[b, r, k : k + 1], gain[l : l + 1])
        return back, row_sums(grad * hat), row_sums(grad)

    def add_sums(l, which, terms):
        for k in range(2):
            total = terms[0][k]
            for term in terms[1:]:
                total = total + term[k]
            m.sums[l, 2 * which + k] += total

    def back_feed(l, s):
        def body(t):
            rows = rows_of(t)
            source = m.cot_in.at[pl.ds(s * nblk, nblk)] if l == layers - 1 else m.dx
            for b, r, _ in parts_of(rows_of(t)):
                m.df[b, r] = source[b, r].astype(BF16)
            m.df_t[:, lanes_of(t)] = flat(m.df[rows]).T
            m.heads_t[:, lanes_of(t)] = flat(m.heads[l, rows]).T
            for half in halves_of(t):
                dg = back_dot(flat(m.df[half]), "w_down", l)
                for b, r, i in parts_of(half):
                    for c in range(hidden // CHUNK):
                        slope = m.slope[l, b, r, cols(c)].astype(F32)
                        m.slope[l, b, r, cols(c)] = (dg[i, cols(c)] * slope).astype(BF16)
            da = back_dot(flat(m.slope[l, rows]), "w_up", l)
            over = 1.0 / gain2[l : l + 1]
            terms = []
            for b, r, i in parts_of(rows_of(t)):
                back, *term = unnorm(l, 1, b, r, da[i], m.a2, gain2, bias2, over)
                terms.append(term)
                dy = source[b, r].astype(F32) + back
                m.dx[b, r] = dy
                m.dm[b, r] = dy.astype(BF16)
            add_sums(l, 1, terms)
            do = back_dot(flat(m.dm[rows]), "w_out", l)
            m.do[pl.ds(t * TILE, TILE)] = blocks(do.astype(BF16))

        loop(tiles, body)

    def back_scores(p, dp):
        parts = []
        for r in pieces_of(dp.shape[0]):
            high = p[r].astype(F32)
            inner = jnp.sum(dp[r] * high, axis=1, keepdims=True)
            parts.append((high * (dp[r] - inner)).astype(BF16))
        return jnp.concatenate(parts, axis=0)

    def back_attend(l, s):
        here = m.qkv.at[l]
        near_p = m.near_p.at[l]

        def body(i):
            near, far = near_tiles(i), far_tiles(i)
            far_do = [flat(m.do[:, spread(j), HEAD:]) for j in far]
            far_p = [m.far_p[l, j] for j in far]
            dp = [dot_nt(m.do[b, :, 0:HEAD], window(here, b, V_NEAR)) for b in near]
            dp += [dot_nt(x, flat(here[:, spread(j), V_FAR])) for j, x in zip(far, far_do)]
            p = [near_p[b] for b in near] + far_p
            ds = [back_scores(x, y) for x, y in zip(p, dp)]
            for b, x in zip(near, ds):
                m.near_ds[b] = x
                m.near_dq[b] = (dot(x, window(here, b, K_NEAR)) * scale).astype(BF16)
            for j, do, w, x in zip(far, far_do, far_p, ds[len(near) :]):
                q = flat(here[:, spread(j), Q_FAR])
                dq = dot(x, flat(here[:, spread(j), K_FAR])) * scale
                dk = dot_tn(x, q) * scale
                dv = dot_tn(w, do)
                here[:, spread(j), Q_FAR] = strided(dq)
                here[:, spread(j), K_FAR] = strided(dk)
                here[:, spread(j), V_FAR] = strided(dv)

        loop(groups // AT_ONCE, body)
        for b in range(nblk):
            if b + 1 < nblk:
                both = slice(b, b + 2)
                ds = jnp.concatenate([m.near_ds[b, :, WINDOW:], m.near_ds[b + 1, :, :WINDOW]], axis=0)
                p = jnp.concatenate([near_p[b, :, WINDOW:], near_p[b + 1, :, :WINDOW]], axis=0)
                q, do = flat(here[both, :, Q_NEAR]), flat(m.do[both, :, 0:HEAD])
            else:
                ds, p = m.near_ds[b, :, WINDOW:], near_p[b, :, WINDOW:]
                q, do = here[b, :, Q_NEAR], m.do[b, :, 0:HEAD]
            here[b, :, K_NEAR] = (dot_tn(ds, q) * scale).astype(BF16)
            here[b, :, V_NEAR] = dot_tn(p, do).astype(BF16)
            here[b, :, Q_NEAR] = m.near_dq[b]

    def back_project(l, s):
        def body(rows):
            da = back_dot(flat(m.qkv[l, rows]), "w_qkv", l)
            over = 1.0 / gain1[l : l + 1]
            terms = []
            for b, r, i in parts_of(rows):
                back, *term = unnorm(l, 0, b, r, da[i], m.a1, gain1, bias1, over)
                terms.append(term)
                if l == 0:
                    m.cot_in[s * nblk + b, r] = (m.dx[b, r] + back).astype(BF16)
                else:
                    m.dx[b, r] = m.dx[b, r] + back
            add_sums(l, 0, terms)

        if roomy:
            body(pl.ds(0, nblk))
        else:
            loop(tiles, lambda t: body(rows_of(t)))

    def outer(l, s, left, ref, first, flipped=False):
        if len(left.shape) == 2:
            product = dot(left[...], flat(ref[...]))
        else:
            product = dot_tn(flat(left[...]), flat(ref[...]))
        for c in range(product.shape[1] // CHUNK):
            part = product[:, cols(c)]
            part = part.T if flipped else part
            if s > 0:
                part = part + m.grad[l, cols(first + c)]
            m.grad[l, cols(first + c)] = part

    def grads_feed(l, s):
        outer(l, s, (m.a2_t if roomy else m.a2).at[l], m.slope.at[l], 0)
        outer(l, s, m.df_t, m.act.at[l], hidden // CHUNK, True)
        outer(l, s, m.heads_t, m.dm, 2 * hidden // CHUNK)

    def grads_attend(l, s):
        outer(l, s, (m.a1_t if roomy else m.a1).at[l], m.qkv.at[l], 2 * hidden // CHUNK + 1)

    core = lax.rem(me, 2)
    second = lax.rem(me // 2, 2)
    bits = nw.bit_length() - 1

    def toggled(bit):
        size = 2**bit
        return me + size - 2 * size * lax.rem(me // size, 2)

    split = 2 * hidden + (CHUNK if CHUNK % (64 * nb) == 0 else 0)

    def reduction(l, which):
        start, count = ((0, split), (split, 12 * CHUNK - split))[which]
        half, chunk, piece = count // 2, count // 2 // nb, count // 4 // nb
        lead = start // 2
        final = m.final.at[l]

        def span(at, size):
            return pl.ds(pl.multiple_of(at, 16), size)

        mine = start + core * half
        theirs = start + (1 - core) * half
        chunk_at = mine + mb * chunk
        piece_at = chunk_at + second * piece
        other_piece = chunk_at + (1 - second) * piece
        core_in = m.got_core.at[l, pl.ds(lead, half)]

        def remote(src, dst, name, k_send, k_recv, device):
            return pltpu.make_async_remote_copy(
                src_ref=src,
                dst_ref=dst,
                send_sem=getattr(m, name + "_s").at[l, which, k_send],
                recv_sem=getattr(m, name + "_r").at[l, which, k_recv],
                device_id=device,
                device_id_type=MESH,
            )

        def here(at, size):
            return final.at[span(at, size)]

        to_core = remote(m.put_core.at[pl.ds(0, half)], core_in, "core", 0, 0, (mb, toggled(0)))
        to_pair = remote(
            m.put_pair.at[pl.ds(start // 4 // nb, piece)],
            m.got_pair.at[l, pl.ds(start // 4 // nb, piece)],
            "pair", 0, 0, (mb, toggled(1)),
        )

        def to_batch(other, owner):
            return remote(
                m.put_batch.at[span(other * chunk, chunk)],
                m.got_batch.at[l, owner, pl.ds(start // 2 // nb, chunk)],
                "batch", other, owner, (other, me),
            )

        def to_top(bit):
            return remote(
                m.put_top.at[bit - 2, pl.ds(start // 4 // nb, piece)],
                m.got_top.at[l, bit - 2, pl.ds(start // 4 // nb, piece)],
                "top", bit - 2, bit - 2, (mb, toggled(bit)),
            )

        def pair_back(at):
            return remote(here(at, piece), here(at, piece), "pair_back", 0, 0, (mb, toggled(1)))

        def batch_back(other, owner):
            at = mine + owner * chunk
            return remote(here(at, chunk), here(at, chunk), "batch_back", other, owner, (other, me))

        def core_back(at):
            return remote(here(at, half), here(at, half), "core_back", 0, 0, (mb, toggled(0)))

        def others():
            return [lax.rem(mb + k, nb) for k in range(1, nb)]

        def step0():
            m.put_core[pl.ds(0, half)] = m.grad[l, span(theirs, half)].astype(BF16)
            to_core.start()

        def step1():
            to_core.wait()
            total = m.grad[l, span(mine, half)] + m.got_core[l, pl.ds(lead, half)].astype(F32)
            m.grad[l, span(mine, half)] = total
            m.put_batch[pl.ds(0, half)] = total.astype(BF16)
            for other in others():
                to_batch(other, mb).start()

        def step2():
            total = m.grad[l, span(chunk_at, chunk)]
            for other in others():
                to_batch(other, mb).wait_send()
                to_batch(other, other).wait_recv()
                got = m.got_batch[l, other, pl.ds(start // 2 // nb, chunk)]
                total = total + got.astype(F32)
            m.grad[l, span(chunk_at, chunk)] = total
            send = m.grad[l, span(other_piece, piece)]
            m.put_pair[pl.ds(start // 4 // nb, piece)] = send.astype(BF16)
            to_pair.start()

        def step3():
            to_pair.wait()
            got = m.got_pair[l, pl.ds(start // 4 // nb, piece)]
            total = m.grad[l, span(piece_at, piece)] + got.astype(F32)
            m.put_top[0, pl.ds(start // 4 // nb, piece)] = total.astype(BF16)
            to_top(2).start()

        def step4(bit=2):
            to_top(bit).wait()
            at = pl.ds(start // 4 // nb, piece)
            total = m.put_top[bit - 2, at].astype(F32) + m.got_top[l, bit - 2, at].astype(F32)
            if bit + 1 < bits:
                m.put_top[bit - 1, at] = total.astype(BF16)
                to_top(bit + 1).start()
                step4(bit + 1)
            else:
                final[span(piece_at, piece)] = total.astype(BF16)
                pair_back(piece_at).start()

        def step5():
            pair_back(other_piece).wait_recv()
            for other in others():
                batch_back(other, mb).start()

        def step6():
            for other in others():
                batch_back(other, other).wait_recv()
            core_back(mine).start()

        save = pltpu.make_async_copy(
            final.at[pl.ds(start, count)],
            grads_hbm.at[l, pl.ds(start, count)],
            m.save.at[l, which],
        )

        def step7():
            core_back(theirs).wait_recv()
            save.start()

        def step8():
            pair_back(piece_at).wait_send()
            for other in others():
                batch_back(other, mb).wait_send()
            core_back(mine).wait_send()
            save.wait()

        return [step0, step1, step2, step3, step4, step5, step6, step7, step8]

    sums = {(l, w): reduction(l, w) for l in range(layers) for w in range(2)}
    waiting = []

    def advance():
        for steps in list(waiting):
            steps.pop(0)()
            if not steps:
                waiting.remove(steps)

    def begin(l, which, last):
        if last:
            steps = sums[l, which]
            steps.pop(0)()
            waiting.append(steps)

    for s in range(ns):
        last = s == ns - 1
        gather_wait(*ins, 0, s, close)
        gather_wait(*ins, 0, s, far[: len(far) // 2])
        if s == 0:
            gather_start(*cots, 1, s)
        gather_wait(*ins, 0, s, far[len(far) // 2 :])
        for l in range(layers):
            with jax.named_scope("layer_forward"):
                forward(l, s)
        gather_wait(*cots, 1, s)
        if not last:
            gather_start(*ins, 0, s + 1)
        else:
            scatter_start(*outs, 2, s)
        for l in reversed(range(layers)):
            with jax.named_scope("feed_backward"):
                back_feed(l, s)
            if l < layers - 1:
                advance()
            with jax.named_scope("feed_gradients"):
                grads_feed(l, s)
            begin(l, 0, last)
            with jax.named_scope("attention_backward"):
                back_attend(l, s)
            advance()
            if not last:
                if l == layers - 1:
                    gather_start(*cots, 1, s + 1)
                if l == 0:
                    scatter_start(*outs, 2, s)
            with jax.named_scope("attention_gradients"):
                grads_attend(l, s)
            begin(l, 1, last)
            with jax.named_scope("input_backward"):
                back_project(l, s)
            if l == 0:
                advance()
        if not last:
            scatter_start(*gis, 3, s)
    scatter_start(*gis, 3, ns - 1, far[: len(far) // 2])
    scatter_start(*gis, 3, ns - 1, close)

    def norm_copy(own, slots, k, device, name, owner):
        return pltpu.make_async_remote_copy(
            src_ref=slots.at[own],
            dst_ref=slots.at[owner],
            send_sem=getattr(m, name + "_s").at[k],
            recv_sem=getattr(m, name + "_r").at[owner],
            device_id=device,
            device_id_type=MESH,
        )

    m.norm_all[me] = jnp.sum(m.sums[...].reshape(4 * layers, 8, width), axis=1)
    for k in range(1, nw):
        other = lax.rem(me + k, nw)
        norm_copy(me, m.norm_all, other, (mb, other), "norm_all", me).start()
    for _ in range(3):
        advance()
    scatter_start(*gis, 3, ns - 1, far[len(far) // 2 :])
    for k in range(1, nw):
        other = lax.rem(me + k, nw)
        norm_copy(me, m.norm_all, other, (mb, other), "norm_all", other).wait_recv()
    total = m.norm_all[0]
    for k in range(1, nw):
        total = total + m.norm_all[k]
    m.norm_batch[mb] = total
    for k in range(1, nb):
        other = lax.rem(mb + k, nb)
        norm_copy(mb, m.norm_batch, other, (other, me), "norm_batch", mb).start()
    while waiting:
        advance()
    for k in range(1, nb):
        other = lax.rem(mb + k, nb)
        norm_copy(mb, m.norm_batch, other, (other, me), "norm_batch", other).wait_recv()
    total = m.norm_batch[0]
    for k in range(1, nb):
        total = total + m.norm_batch[k]
    norm_out[...] = total

    for k in range(1, nw):
        other = lax.rem(me + k, nw)
        norm_copy(me, m.norm_all, other, (mb, other), "norm_all", me).wait_send()
    for k in range(1, nb):
        other = lax.rem(mb + k, nb)
        norm_copy(mb, m.norm_batch, other, (other, me), "norm_batch", mb).wait_send()
    for s in range(ns):
        gather_end(*ins, s)
        gather_end(*cots, s)
        scatter_end(*outs, 2, s)
        scatter_end(*gis, 3, s)


def per_device(nb, nw, inputs, lengths, gain1, bias1, w_qkv, w_out, gain2, bias2, w_up, w_down, cotangent):
    count, block, width = inputs.shape
    layers, _, hidden = w_up.shape
    ns, per = count // nw, block // WINDOW
    pieces = plan(nb, nw, ns, nw * per, width, hidden, layers)
    shape = (nw, ns, per, WINDOW, width)
    anywhere = pl.BlockSpec(memory_space=pl.ANY)
    vmem = pl.BlockSpec(memory_space=pltpu.VMEM)
    rows = 12 * CHUNK

    def body(*refs):
        kernel(nb, nw, ns, list(pieces), *refs)

    outputs, grad_rows, grads, norms = pl.pallas_call(
        body,
        out_shape=(
            jax.ShapeDtypeStruct(shape, BF16),
            jax.ShapeDtypeStruct(shape, BF16),
            jax.ShapeDtypeStruct((layers, rows, CHUNK), BF16),
            jax.ShapeDtypeStruct((4 * layers, width), F32),
        ),
        in_specs=[pl.BlockSpec(memory_space=pltpu.SMEM)] + [anywhere] * 2 + [vmem] * 4 + [anywhere] * 4,
        out_specs=(anywhere, anywhere, anywhere, vmem),
        scratch_shapes=list(pieces.values()),
        compiler_params=pltpu.CompilerParams(
            collective_id=0, has_side_effects=True, vmem_limit_bytes=64 * 1024 * 1024
        ),
    )(
        lengths, inputs.reshape(shape), cotangent.reshape(shape),
        gain1, bias1, gain2, bias2, w_qkv, w_out, w_up, w_down,
    )
    each = hidden // CHUNK
    tokens = count * block // layers

    def finish(out_in, rows_in, grads_in, norm_in, *results):
        out_out, rows_out, qkv_out, rest_out, up_out, down_out, *norm_outs = results
        out_out[...] = out_in[...]
        rows_out[...] = rows_in[...].astype(F32)

        def part(c):
            return grads_in[0, c * CHUNK : (c + 1) * CHUNK].astype(F32)

        for c in range(each):
            up_out[0, :, c * CHUNK : (c + 1) * CHUNK] = part(c)
            down_out[0, c * CHUNK : (c + 1) * CHUNK] = part(each + c)
        rest_out[0] = part(2 * each)
        for c in range(3):
            qkv_out[0, :, c * CHUNK : (c + 1) * CHUNK] = part(2 * each + 1 + c)
        for l in range(layers):
            for k in range(4):
                norm_outs[k][l : l + 1] = norm_in[4 * l + k : 4 * l + k + 1]

    row_spec = pl.BlockSpec((tokens, width), lambda i: (i, 0))
    norm_spec = pl.BlockSpec((layers, width), lambda i: (0, 0))

    def layer_spec(*dims):
        return pl.BlockSpec((1, *dims), lambda i: (i, 0, 0))

    outputs, grad_rows, grad_qkv, grad_out, grad_up, grad_down, *norms = pl.pallas_call(
        finish,
        grid=(layers,),
        out_shape=(
            jax.ShapeDtypeStruct((count * block, width), BF16),
            jax.ShapeDtypeStruct((count * block, width), F32),
            jax.ShapeDtypeStruct((layers, width, 3 * width), F32),
            jax.ShapeDtypeStruct((layers, width, width), F32),
            jax.ShapeDtypeStruct((layers, width, hidden), F32),
            jax.ShapeDtypeStruct((layers, hidden, width), F32),
        )
        + (jax.ShapeDtypeStruct((layers, width), F32),) * 4,
        in_specs=[
            row_spec,
            row_spec,
            layer_spec(rows, CHUNK),
            pl.BlockSpec((4 * layers, width), lambda i: (0, 0)),
        ],
        out_specs=(
            row_spec,
            row_spec,
            layer_spec(width, 3 * width),
            layer_spec(width, width),
            layer_spec(width, hidden),
            layer_spec(hidden, width),
        )
        + (norm_spec,) * 4,
        compiler_params=pltpu.CompilerParams(vmem_limit_bytes=60 * 1024 * 1024),
    )(outputs.reshape(count * block, width), grad_rows.reshape(count * block, width), grads, norms)
    return (
        outputs.reshape(count, block, width),
        grad_rows.reshape(count, block, width),
        norms[0],
        norms[1],
        grad_qkv,
        grad_out,
        norms[2],
        norms[3],
        grad_up,
        grad_down,
    )


def solution(mesh):
    nb, nw = mesh.shape["batch"], mesh.shape["wide"]

    def step(*args):
        return per_device(nb, nw, *args)

    rows = P("batch", "wide", None)
    return jax.shard_map(
        step,
        mesh=mesh,
        in_specs=(rows, P("batch")) + (P(),) * 8 + (rows,),
        out_specs=(rows, rows) + (P(),) * 8,
        check_vma=False,
    )
```
